32 devices in a mesh: pipe: 4 (over y, x), expert: 8 (over z, core).
Axes of the slice: x: 2, y: 2, z: 4, core: 2. Of those that a mesh axis runs over, the one named last changes fastest.
Arguments:
- fwd_state: bfloat16 [4, 512, 3584], P('pipe', 'expert'), may hold values from -6 to 6
- rev_state: bfloat16 [4, 512, 3584], P('pipe', 'expert'), may hold values from -6 to 6
- norm_gain: float32 [4, 3584], P('pipe'), may hold values from 0.5 to 1.5
- w_gate: bfloat16 [4, 3584, 1024], P('pipe', None, 'expert'), may hold values from -0.09375 to 0.09375
- w_up: bfloat16 [4, 3584, 1024], P('pipe', None, 'expert'), may hold values from -0.09375 to 0.09375
- w_down: bfloat16 [4, 1024, 3584], P('pipe', 'expert'), may hold values from -0.1875 to 0.1875
- routes_fwd: int32 [3, 4, 512, 8], P(None, 'pipe', 'expert'), may hold values from 0 to 255, as said below
- scores_fwd: float32 [3, 4, 512, 8], P(None, 'pipe', 'expert'), may hold values from 0.02 to 1
- routes_rev: int32 [3, 4, 512, 8], P(None, 'pipe', 'expert'), may hold values from 0 to 255, as said below
- scores_rev: float32 [3, 4, 512, 8], P(None, 'pipe', 'expert'), may hold values from 0.02 to 1
Outputs:
- fwd_out: bfloat16 [4, 512, 3584], P('pipe', 'expert')
- rev_out: bfloat16 [4, 512, 3584], P('pipe', 'expert')
The draws below stay inside these ranges and needn't reach their ends.
Inputs may be any that keep to these rules, and one draw needn't show every extreme that they name: `routes_fwd`: each row names 8 different experts, all from at most 4 of the 8 groups of 32 consecutive experts. Among the 64 rows of one device, each expert below 1 is named by 1 to 4 rows, and one of them by exactly 4. `routes_rev`: as for routes_fwd.
All inputs are finite; a program needn't handle non-finite values.
Results may differ from the reference program's by a relative error of at most 0.003.
Values may be sent and summed in bfloat16 or wider, within the bound.
A program may use at most 64 MiB of HBM per device.

```python
import functools
import math
import jax
import jax.numpy as jnp
from jax import lax

D = 3584
MOE_FF = 1024
N_ALL = 256
GROUPS = 8
TOPG = 4
TOPK = 8
SPLIT = 8
CAP = 4
STEPS = 3
TOK_DEV = 64
TOKENS = 512
HID_DEV = 128
E_FLY = 1
N_PIPE = 4
N_EXPERT = 8


def block_routes(key):
    key_list = jax.random.split(key, 5)
    busiest = jax.random.randint(key_list[0], (), 0, E_FLY)
    counts = jax.random.randint(key_list[1], (E_FLY,), 1, CAP // 2 + 1)
    counts = jnp.where(jnp.arange(E_FLY) == busiest, CAP, counts)
    row_draw = jax.random.randint(key_list[2], (E_FLY, TOK_DEV), 0, 1 << 20)
    row_score = row_draw * TOK_DEV + jnp.arange(TOK_DEV, dtype=jnp.int32)[None, :]
    row_rank = jnp.argsort(jnp.argsort(row_score, axis=1), axis=1)
    hit_mask = row_rank < counts[:, None]
    any_hit = jnp.any(hit_mask, axis=0)
    group_ids = jnp.arange(GROUPS, dtype=jnp.int32)
    group_score = jax.random.randint(key_list[3], (TOK_DEV, GROUPS), 0, 1 << 20) * GROUPS + group_ids[None, :]
    group_score = group_score + jnp.where(any_hit[:, None] & (group_ids[None, :] == 0), 1 << 26, 0)
    group_rank = jnp.argsort(jnp.argsort(-group_score, axis=1), axis=1)
    chosen = group_rank < TOPG
    in_group = jnp.repeat(chosen, N_ALL // GROUPS, axis=1)
    expert_ids = jnp.arange(N_ALL, dtype=jnp.int32)
    base_score = jax.random.randint(key_list[4], (TOK_DEV, N_ALL), 0, 1 << 20) * N_ALL + expert_ids[None, :]
    hit_full = jnp.concatenate([hit_mask.T, jnp.zeros((TOK_DEV, N_ALL - E_FLY), dtype=bool)], axis=1)
    is_flying = expert_ids[None, :] < E_FLY
    final_score = jnp.where(is_flying, jnp.where(hit_full, (1 << 29) + expert_ids[None, :], -1), jnp.where(in_group, base_score, -1))
    picks = jnp.argsort(-final_score, axis=1)[:, :TOPK]
    return picks.astype(jnp.int32)


def all_routes(key, salt):
    key_list = jax.random.split(jax.random.fold_in(key, salt), STEPS * N_PIPE * N_EXPERT)
    drawn = jax.vmap(block_routes)(key_list)
    return drawn.reshape(STEPS, N_PIPE, N_EXPERT * TOK_DEV, TOPK)


def draw_routes_fwd(key, part):
    return all_routes(key, 11)


def draw_routes_rev(key, part):
    return all_routes(key, 23)


def levels(own_key, dims, cuts, least, high):
    def one(position, shards_of):
        steps = jax.random.uniform(jax.random.fold_in(jax.random.fold_in(own_key, 6), position), (shards_of,), jnp.float32, least / len(cuts), high / len(cuts))
        return jnp.repeat(jnp.exp(steps), dims[position] // shards_of).reshape((-1,) + (1,) * (len(dims) - position - 1))

    loudness = one(*cuts[0])
    for cut in cuts[1:]:
        loudness = loudness * one(*cut)
    return loudness


def centred(own_key, extent, width, bound, cuts=(), kind=jnp.bfloat16):
    array = jax.random.normal(own_key, extent, jnp.float32) * width
    if len(cuts) > 0:
        array = levels(own_key, extent, cuts, -0.22, 0.18) * array
    return jnp.clip(array, min=-bound, max=bound).astype(kind)


def setup_inputs(seed: int = 0) -> dict:
    arg_keys = jax.random.split(jax.random.key(seed), 11)
    fwd_state = centred(arg_keys[0], (N_PIPE, TOKENS, D), 1.0, 6.0, ((0, 4), (1, 8)))
    rev_state = centred(arg_keys[1], (N_PIPE, TOKENS, D), 1.0, 6.0, ((0, 4), (1, 8)))
    norm_gain = jnp.clip(1.0 + 0.1 * jax.random.normal(arg_keys[2], (N_PIPE, D), jnp.float32), 0.5, 1.5)
    w_gate = centred(arg_keys[3], (N_PIPE, D, E_FLY * MOE_FF), D ** -0.5, 0.09375, ((0, 4), (2, 8)))
    w_up = centred(arg_keys[4], (N_PIPE, D, E_FLY * MOE_FF), D ** -0.5, 0.09375, ((0, 4), (2, 8)))
    w_down = centred(arg_keys[5], (N_PIPE, E_FLY * MOE_FF, D), MOE_FF ** -0.5, 0.1875, ((0, 4), (1, 8)))
    routes_fwd = draw_routes_fwd(jax.random.fold_in(arg_keys[10], 71), 0)
    scores_fwd = jnp.clip(jnp.exp(math.log(1.0) - 3.912023 * jax.random.uniform(arg_keys[7], (STEPS, N_PIPE, TOKENS, TOPK), jnp.float32) ** levels(arg_keys[7], (STEPS, N_PIPE, TOKENS, TOPK), ((1, 4), (2, 8)), -0.2, 0.2)), 0.02, 1.0)
    routes_rev = draw_routes_rev(jax.random.fold_in(arg_keys[10], 71), 0)
    scores_rev = jnp.clip(jnp.exp(math.log(1.0) - 3.912023 * jax.random.uniform(arg_keys[9], (STEPS, N_PIPE, TOKENS, TOPK), jnp.float32) ** levels(arg_keys[9], (STEPS, N_PIPE, TOKENS, TOPK), ((1, 4), (2, 8)), -0.2, 0.2)), 0.02, 1.0)
    return {"fwd_state": fwd_state, "rev_state": rev_state, "norm_gain": norm_gain, "w_gate": w_gate, "w_up": w_up, "w_down": w_down, "routes_fwd": routes_fwd, "scores_fwd": scores_fwd, "routes_rev": routes_rev, "scores_rev": scores_rev}


EPSILON = 1e-06
ROUTE_SCALE = 2.5

def normalize(tok_rows, gain_row):
    values = tok_rows.astype(jnp.float32)
    factor = lax.rsqrt(lax.optimization_barrier(jnp.mean(values * values, axis=-1, keepdims=True)) + EPSILON)
    return (values * factor * gain_row).astype(jnp.bfloat16)

def slot_tables(route_ids, route_scores, flying):
    expert_ids = jnp.arange(flying, dtype=jnp.int32)
    matches = (route_ids[:, :, None] == expert_ids[None, None, :]).astype(jnp.float32)
    hit_mask = lax.optimization_barrier(jnp.sum(matches, axis=1))
    weighted = ROUTE_SCALE * lax.optimization_barrier(jnp.sum(matches * route_scores[:, :, None], axis=1)) / lax.optimization_barrier(jnp.sum(route_scores, axis=1, keepdims=True))
    slot_index = jnp.cumsum(hit_mask, axis=0) - 1.0
    slot_ids = jnp.arange(CAP, dtype=jnp.float32)
    placed = hit_mask.T[:, None, :] * (slot_index.T[:, None, :] == slot_ids[None, :, None]).astype(jnp.float32)
    mix_table = placed * weighted.T[:, None, :]
    return (placed, mix_table)

def dispatch_slots(normed, placed):
    return jnp.einsum('ecr,rd->ecd', placed, normed.astype(jnp.float32), precision=lax.Precision.HIGHEST).astype(jnp.bfloat16)

def finish(tok_rows, summed, mix_table):
    added = jnp.einsum('ecr,ecd->rd', mix_table, summed, precision=lax.Precision.HIGHEST)
    return (tok_rows.astype(jnp.float32) + added).astype(jnp.bfloat16)

def section_layer(current, gain_row, gate_cols, up_cols, down_rows, route_ids, route_scores):
    blocks = current.reshape(N_EXPERT, TOK_DEV, D)
    id_blocks = route_ids.reshape(N_EXPERT, TOK_DEV, TOPK)
    score_blocks = route_scores.reshape(N_EXPERT, TOK_DEV, TOPK)
    normed = jax.vmap(normalize, in_axes=(0, None))(blocks, gain_row)
    placed, mix_table = jax.vmap(functools.partial(slot_tables, flying=E_FLY))(id_blocks, score_blocks)
    slot_rows = jax.vmap(dispatch_slots)(normed, placed)
    summed_list = []
    for expert in range(E_FLY):
        chosen = slot_rows[:, expert].reshape(N_EXPERT * CAP, D)
        lowest = expert * MOE_FF
        gate_act = jnp.dot(chosen, gate_cols[:, lowest:lowest + MOE_FF], preferred_element_type=jnp.float32)
        up_act = jnp.dot(chosen, up_cols[:, lowest:lowest + MOE_FF], preferred_element_type=jnp.float32)
        hidden = (jax.nn.silu(gate_act) * up_act).astype(jnp.bfloat16)
        down_part = down_rows[lowest:lowest + MOE_FF].reshape(SPLIT, HID_DEV, D).astype(jnp.float32)
        pieces = jnp.einsum('rsh,shd->rsd', hidden.reshape(N_EXPERT * CAP, SPLIT, HID_DEV).astype(jnp.float32), down_part)
        rounded = lax.optimization_barrier(pieces.astype(jnp.bfloat16))
        summed = lax.optimization_barrier(jnp.sum(rounded.astype(jnp.float32), axis=1))
        summed_list.append(summed.reshape(N_EXPERT, CAP, D))
    summed_all = jnp.stack(summed_list, axis=1)
    out_blocks = jax.vmap(finish)(blocks, summed_all, mix_table)
    return out_blocks.reshape(TOKENS, D)

def reference(fwd_state, rev_state, norm_gain, w_gate, w_up, w_down, routes_fwd, scores_fwd, routes_rev, scores_rev):

    def run_sections(states, route_ids, route_scores):

        def apply_section(packed):
            return section_layer(*packed)
        return lax.map(apply_section, (states, norm_gain, w_gate, w_up, w_down, route_ids, route_scores))
    forward_now = fwd_state
    reverse_now = rev_state
    for step_index in range(STEPS):
        forward_now = jnp.roll(run_sections(forward_now, routes_fwd[step_index], scores_fwd[step_index]), 1, axis=0)
        reverse_now = jnp.roll(run_sections(reverse_now, routes_rev[step_index], scores_rev[step_index]), -1, axis=0)
    return (forward_now, reverse_now)
```

```python
import jax
import jax.numpy as jnp
from jax import lax
from jax.experimental import pallas as pl
from jax.experimental.pallas import tpu as pltpu
from jax.sharding import PartitionSpec as P

SPLIT = 8
CAP = 4
STEPS = 3
PARTS = 4
CHUNKS = 4

EPSILON = 1e-06
ROUTE_SCALE = 2.5
MESH = pl.DeviceIdType.MESH


def shifted(value, axis, steps):
    count = lax.axis_size(axis)
    pairs = [(source, (source + steps) % count) for source in range(count)]
    return lax.ppermute(value, axis, pairs)


def normalize(tok_rows, gain_row):
    values = tok_rows.astype(jnp.float32)
    factor = lax.rsqrt(jnp.mean(values * values, axis=-1, keepdims=True) + EPSILON)
    return (values * factor * gain_row).astype(jnp.bfloat16)


def slot_tables(route_ids, route_scores, flying):
    expert_ids = jnp.arange(flying, dtype=jnp.int32)
    matches = (route_ids[:, :, None] == expert_ids[None, None, :]).astype(jnp.float32)
    hit_mask = jnp.sum(matches, axis=1)
    weighted = (
        ROUTE_SCALE
        * jnp.sum(matches * route_scores[:, :, None], axis=1)
        / jnp.sum(route_scores, axis=1, keepdims=True)
    )
    slot_index = jnp.cumsum(hit_mask, axis=0) - 1.0
    slot_ids = jnp.arange(CAP, dtype=jnp.float32)
    placed = hit_mask.T[:, None, :] * (slot_index.T[:, None, :] == slot_ids[None, :, None]).astype(
        jnp.float32
    )
    mix_table = placed * weighted.T[:, None, :]
    return (placed, mix_table)


def dispatch_slots(normed, placed):
    return jnp.einsum(
        "ecr,rd->ecd", placed, normed.astype(jnp.float32), precision=lax.Precision.HIGHEST
    ).astype(jnp.bfloat16)


def finish(tok_rows, summed, mix_table):
    added = jnp.einsum("ecr,ecd->rd", mix_table, summed, precision=lax.Precision.HIGHEST)
    return (tok_rows.astype(jnp.float32) + added).astype(jnp.bfloat16)


def general_local(
    fwd_state,
    rev_state,
    norm_gain,
    w_gate,
    w_up,
    w_down,
    routes_fwd,
    scores_fwd,
    routes_rev,
    scores_rev,
):
    flying = lax.axis_size("expert") // SPLIT
    width = fwd_state.shape[2]
    gain_row = norm_gain[0]
    gate_cols = w_gate[0]
    up_cols = w_up[0]
    down_rows = w_down[0]

    def prepare(current, route_ids, route_scores):
        normed = normalize(current[0], gain_row)
        placed, mix_table = slot_tables(route_ids, route_scores, flying)
        slot_rows = dispatch_slots(normed, placed)
        copies = jnp.broadcast_to(slot_rows[:, None], (flying, SPLIT, CAP, width)).reshape(
            flying * SPLIT, CAP, width
        )
        return (copies, mix_table)

    def finish_stream(current, returned, mix_table):
        summed = jnp.sum(returned.astype(jnp.float32).reshape(flying, SPLIT, CAP, width), axis=1)
        return finish(current[0], summed, mix_table)[None]

    forward_now = fwd_state
    reverse_now = rev_state
    for step_index in range(STEPS):
        fwd_copies, fwd_mix = prepare(
            forward_now, routes_fwd[step_index, 0], scores_fwd[step_index, 0]
        )
        rev_copies, rev_mix = prepare(
            reverse_now, routes_rev[step_index, 0], scores_rev[step_index, 0]
        )
        joined = jnp.concatenate([fwd_copies, rev_copies], axis=1)
        received = lax.all_to_all(joined, "expert", split_axis=0, concat_axis=0, tiled=True)
        tok_rows = received.reshape(-1, width)
        gate_act = jnp.dot(tok_rows, gate_cols, preferred_element_type=jnp.float32)
        up_act = jnp.dot(tok_rows, up_cols, preferred_element_type=jnp.float32)
        hidden = (jax.nn.silu(gate_act) * up_act).astype(jnp.bfloat16)
        partial_out = jnp.dot(hidden, down_rows, preferred_element_type=jnp.float32).astype(
            jnp.bfloat16
        )
        returned = lax.all_to_all(
            partial_out.reshape(received.shape), "expert", split_axis=0, concat_axis=0, tiled=True
        )
        fwd_back = returned[:, :CAP]
        rev_back = returned[:, CAP:]
        forward_now = shifted(finish_stream(forward_now, fwd_back, fwd_mix), "pipe", 1)
        reverse_now = shifted(finish_stream(reverse_now, rev_back, rev_mix), "pipe", -1)
    return (forward_now, reverse_now)


def relay_kernel(
    fwd_ref,
    rev_ref,
    gain_ref,
    route_ref,
    score_ref,
    gate_hbm,
    up_hbm,
    down_hbm,
    fwd_out,
    rev_out,
    gate_up,
    down,
    table,
    table_in,
    early_out,
    early_in,
    slots,
    pieces,
    mate_pieces,
    chip_sums,
    returned,
    changed,
    changed_in,
    bulk_in,
    weight_sem,
    table_send,
    table_recv,
    early_send,
    early_recv,
    slot_send,
    slot_recv,
    piece_send,
    piece_recv,
    back_send,
    back_recv,
    changed_send,
    changed_recv,
    bulk_send,
    bulk_recv,
):
    f32, bf16 = jnp.float32, jnp.bfloat16
    states = (fwd_ref, rev_ref)
    tokens, width = fwd_ref.shape[1], fwd_ref.shape[2]
    part = width // PARTS
    rows = PARTS * CAP
    sections = lax.axis_size("pipe")
    holders = lax.axis_size("expert")
    me_pipe = lax.axis_index("pipe")
    me_expert = lax.axis_index("expert")
    chips = holders // 2
    core = lax.rem(me_expert, 2)
    chip = me_expert // 2

    def at_section(offset):
        return {"pipe": lax.rem(me_pipe + sections + offset, sections)}

    def at_chip(offset):
        return {"expert": lax.rem(chip + chips + offset, chips) * 2 + core}

    mate = {"expert": chip * 2 + 1 - core}

    unsent = []

    def remote(source, target, send, recv, device):
        return pltpu.make_async_remote_copy(
            src_ref=source,
            dst_ref=target,
            send_sem=send,
            recv_sem=recv,
            device_id=device,
            device_id_type=MESH,
        )

    def launch(copy):
        copy.start()
        unsent.append(copy)

    barrier = pltpu.get_barrier_semaphore()
    peers = [at_section(d) for d in range(1, 4)] + [at_chip(k) for k in range(1, chips)] + [mate]
    for peer in peers:
        pl.semaphore_signal(barrier, inc=1, device_id=peer, device_id_type=MESH)

    weight_copies = [
        pltpu.make_async_copy(gate_hbm.at[0], gate_up.at[:, 0:128], weight_sem.at[0]),
        pltpu.make_async_copy(up_hbm.at[0], gate_up.at[:, 128:256], weight_sem.at[1]),
        pltpu.make_async_copy(down_hbm.at[0], down, weight_sem.at[2]),
    ]
    for copy in weight_copies:
        copy.start()

    lanes = 128
    before = (
        lax.broadcasted_iota(jnp.int32, (lanes, lanes), 0)
        <= lax.broadcasted_iota(jnp.int32, (lanes, lanes), 1)
    ).astype(f32)
    slot_of_row = lax.rem(lax.broadcasted_iota(jnp.int32, (8, lanes), 0), CAP).astype(f32)
    mix = {}
    for stream in range(2):
        for step in range(STEPS):
            match = (route_ref[stream, step] == 0).astype(f32)
            score = score_ref[stream, step]
            hit = jnp.sum(match, axis=0, keepdims=True)
            weighted = (
                ROUTE_SCALE
                * jnp.sum(match * score, axis=0, keepdims=True)
                / jnp.sum(score, axis=0, keepdims=True)
            )
            hits = jnp.broadcast_to(hit, (8, lanes))
            place = jnp.dot(hits, before, preferred_element_type=f32) - 1.0
            placed = hits * (place == slot_of_row).astype(f32)
            table[stream, step] = placed
            column = jnp.sum(placed * weighted, axis=1, keepdims=True)
            mix[stream, step] = jnp.concatenate([column, column], axis=0)

    part_of_row = lax.broadcasted_iota(jnp.int32, (rows, part), 0) // CAP

    def by_part(pick):
        total = pick(PARTS - 1)
        for q in range(PARTS - 1):
            total = jnp.where(part_of_row == q, pick(q), total)
        return total

    def cols(q):
        return slice(q * part, (q + 1) * part)

    def twice(placed):
        return jnp.concatenate([placed, placed], axis=0)

    def select(placed, state):
        marks = twice(placed)[:, :tokens].astype(bf16)
        return by_part(
            lambda q: jnp.dot(marks, state[0, :, cols(q)], preferred_element_type=f32)
        )

    gain = by_part(lambda q: jnp.broadcast_to(gain_ref[:, cols(q)], (rows, part)))

    def table_copy(d):
        return remote(
            table, table_in.at[d - 1], table_send.at[d - 1], table_recv.at[d - 1], at_section(d)
        )

    def sign(stream):
        return 1 if stream == 0 else -1

    def table_from(stream, behind):
        offset = behind if stream == 0 else (-behind) % 4
        return table_in.at[offset - 1, stream]

    def early_copy(stream, d):
        return remote(
            early_out.at[stream, d - 1],
            early_in.at[stream, d - 1],
            early_send.at[stream, d - 1],
            early_recv.at[stream, d - 1],
            at_section(sign(stream) * d),
        )

    def bulk_copy(stream, chunk):
        size = tokens // CHUNKS
        piece = pl.ds(chunk * size, size)
        return remote(
            states[stream].at[0, piece],
            bulk_in.at[stream, piece],
            bulk_send.at[stream, chunk],
            bulk_recv.at[stream, chunk],
            at_section(sign(stream) * 3),
        )

    def changed_copy(stream, step, d):
        return remote(
            changed.at[stream, step],
            changed_in.at[stream, step, d - 1],
            changed_send.at[stream, step, d - 1],
            changed_recv.at[stream, step, d - 1],
            at_section(sign(stream) * d),
        )

    def slot_copy(stream, step, k):
        return remote(
            slots.at[stream, step, 0],
            slots.at[stream, step, k],
            slot_send.at[stream, step, k],
            slot_recv.at[stream, step, k],
            at_chip(k),
        )

    def mate_copy(stream, step, k):
        return remote(
            slots.at[stream, step, k],
            slots.at[stream, step, chips + k],
            slot_send.at[stream, step, chips + k],
            slot_recv.at[stream, step, chips + k],
            mate,
        )

    def piece_copy(stream, step):
        return remote(
            pieces.at[stream, step, 1],
            mate_pieces.at[stream, step],
            piece_send.at[stream, step],
            piece_recv.at[stream, step],
            mate,
        )

    def back_copy(stream, step, k):
        return remote(
            chip_sums.at[stream, step, k],
            returned.at[stream, step, k - 1],
            back_send.at[stream, step, k - 1],
            back_recv.at[stream, step, k - 1],
            at_chip(-k),
        )

    row_part = lax.broadcasted_iota(jnp.int32, (rows, rows), 0) // CAP
    col_part = lax.broadcasted_iota(jnp.int32, (rows, rows), 1) // CAP
    same_part = (row_part == col_part).astype(f32)

    def chain(stream):
        for step in range(STEPS):
            own = table[stream, step]
            if step == 0:
                current = select(own, states[stream])
            else:
                early_copy(stream, step).wait_recv()
                current = early_in[stream, step - 1].astype(f32)
                for past in range(step):
                    behind = step - past
                    match = same_part * lax.dot_general(
                        twice(own),
                        twice(table_from(stream, behind)[past]),
                        (((1,), (1,)), ((), ())),
                        preferred_element_type=f32,
                    )
                    seen = jnp.sum(match, axis=1, keepdims=True)
                    changed_copy(stream, past, behind).wait_recv()
                    newer = jnp.dot(
                        match.astype(bf16),
                        changed_in[stream, past, behind - 1],
                        preferred_element_type=f32,
                    )
                    current = jnp.where(seen > 0.5, newer, current)
            squares = jnp.sum(current * current, axis=1, keepdims=True)
            squares = jnp.broadcast_to(squares, (rows, 128))
            squares = squares[:8] + squares[8:]
            squares = squares + pltpu.roll(squares, 4, 0)
            factor = lax.rsqrt(squares[:, :1] * (1.0 / width) + EPSILON)
            slots[stream, step, 0] = (current * twice(factor) * gain).astype(bf16)
            if step == 0 and stream == 0:
                pl.semaphore_wait(barrier, len(peers))
            for k in (2, 1, 3):
                launch(slot_copy(stream, step, k))
            launch(mate_copy(stream, step, 0))
            yield
            for k in (1, 3, 2):
                slot_copy(stream, step, k).wait_recv()
                launch(mate_copy(stream, step, k))
            yield
            for k in range(chips):
                mate_copy(stream, step, k).wait_recv()
            if step == 0 and stream == 0:
                for copy in weight_copies:
                    copy.wait()
            gathered = slots[stream, step].reshape(holders * rows, part)
            total = None
            part_of_line = (
                lax.broadcasted_iota(jnp.int32, (holders * rows, 256), 0) % rows
            ) // CAP
            for q in range(PARTS):
                product = jnp.dot(gathered, gate_up[cols(q), :], preferred_element_type=f32)
                total = product if q == 0 else jnp.where(part_of_line == q, product, total)
            total = total.reshape(holders, 2, 8, 256)
            total = total[:, 0] + total[:, 1]
            total = (total + pltpu.roll(total, 4, 1)).reshape(holders * 8, 256)
            gate_act, up_act = total[:, :128], total[:, 128:]
            hidden = (gate_act / (1.0 + jnp.exp(-gate_act)) * up_act).astype(bf16)
            low = lax.broadcasted_iota(jnp.int32, (holders * 8, part), 0) % 8 < CAP
            halves = []
            for half in range(2):
                one = jnp.dot(hidden, down[:, cols(2 * half)], preferred_element_type=f32)
                two = jnp.dot(hidden, down[:, cols(2 * half + 1)], preferred_element_type=f32)
                halves.append(jnp.where(low, one, two).reshape(holders, 1, 8, part))
            joined = jnp.concatenate(halves, axis=1).reshape(2, chips, rows, part)
            pieces[stream, step] = joined.astype(bf16)
            launch(piece_copy(stream, step))
            yield
            piece_copy(stream, step).wait_recv()
            sums = pieces[stream, step, 0].astype(f32) + mate_pieces[stream, step].astype(f32)
            chip_sums[stream, step] = sums.astype(bf16)
            for k in (2, 1, 3):
                launch(back_copy(stream, step, k))
            yield
            expert_out = sums[0]
            for k in range(1, chips):
                back_copy(stream, step, k).wait_recv()
                expert_out = expert_out + returned[stream, step, k - 1].astype(f32)
            changed[stream, step] = (current + mix[stream, step] * expert_out).astype(bf16)
            for d in range(1, STEPS - step + 1):
                launch(changed_copy(stream, step, d))

    def tables_out():
        for d in range(1, 4):
            launch(table_copy(d))

    def early_rows():
        for d in range(1, 4):
            table_copy(d).wait_recv()
        for stream in range(2):
            for d in range(1, STEPS):
                ahead = table_from(stream, 4 - d)
                early_out[stream, d - 1] = select(ahead[d], states[stream]).astype(bf16)
                launch(early_copy(stream, d))

    def bulk(chunk):
        for stream in range(2):
            launch(bulk_copy(stream, chunk))

    extras = {
        0: [tables_out],
        1: [early_rows, lambda: bulk(0)],
        3: [lambda: bulk(1)],
        5: [lambda: bulk(2)],
        7: [lambda: bulk(3)],
    }
    chains = [chain(0), chain(1)]
    turn = 0
    while chains:
        for one in list(chains):
            try:
                next(one)
            except StopIteration:
                chains.remove(one)
        for extra in extras.get(turn, []):
            extra()
        turn += 1

    slot_lane = lax.broadcasted_iota(jnp.int32, (tokens, lanes), 1)
    for stream, out in ((0, fwd_out), (1, rev_out)):
        marks = []
        for step in range(STEPS):
            placed = table_from(stream, STEPS - step)[step]
            for later in range(step + 1, STEPS):
                newer = table_from(stream, STEPS - later)[later]
                placed = placed * (1.0 - jnp.sum(newer[:CAP], axis=0, keepdims=True))
            marks.append(twice(placed))
        marks.append(jnp.zeros((lanes - STEPS * rows, lanes), f32))
        spread = jnp.concatenate(marks, axis=0).T[:tokens]
        seen = jnp.sum(spread, axis=1, keepdims=True) > 0.5
        for chunk in range(CHUNKS):
            bulk_copy(stream, chunk).wait_recv()
        for step in range(STEPS):
            changed_copy(stream, step, STEPS - step).wait_recv()
        newest = [changed_in[stream, step, STEPS - step - 1] for step in range(STEPS)]
        newest.append(jnp.zeros((lanes - STEPS * rows, part), bf16))
        newest = jnp.concatenate(newest, axis=0)
        for q in range(PARTS):
            chosen = jnp.where(lax.rem(slot_lane, rows) // CAP == q, spread, 0.0).astype(bf16)
            newer = jnp.dot(chosen, newest, preferred_element_type=f32)
            older = bulk_in[stream, :, cols(q)].astype(f32)
            out[0, :, cols(q)] = jnp.where(seen, newer, older).astype(bf16)

    for copy in unsent:
        copy.wait_send()


def relay_local(
    fwd_state,
    rev_state,
    norm_gain,
    w_gate,
    w_up,
    w_down,
    routes_fwd,
    scores_fwd,
    routes_rev,
    scores_rev,
):
    tokens, width = fwd_state.shape[1:]
    part = width // PARTS
    rows = PARTS * CAP
    holders = SPLIT
    chips = holders // 2
    bf16 = jnp.bfloat16

    def across(first, second, fill):
        both = jnp.stack([first[:, 0], second[:, 0]]).transpose(0, 1, 3, 2)
        return jnp.pad(both, ((0, 0), (0, 0), (0, 0), (0, 128 - tokens)), constant_values=fill)

    routes = across(routes_fwd, routes_rev, -1)
    scores = across(scores_fwd, scores_rev, 1.0)
    vmem = pl.BlockSpec(memory_space=pltpu.VMEM)
    anywhere = pl.BlockSpec(memory_space=pl.ANY)
    dma = pltpu.SemaphoreType.DMA
    return pl.pallas_call(
        relay_kernel,
        out_shape=[jax.ShapeDtypeStruct(fwd_state.shape, bf16)] * 2,
        in_specs=[vmem] * 5 + [anywhere] * 3,
        out_specs=[vmem, vmem],
        scratch_shapes=[
            pltpu.VMEM((width, 256), bf16),
            pltpu.VMEM((128, width), bf16),
            pltpu.VMEM((2, STEPS, 8, 128), jnp.float32),
            pltpu.VMEM((3, 2, STEPS, 8, 128), jnp.float32),
            pltpu.VMEM((2, STEPS - 1, rows, part), bf16),
            pltpu.VMEM((2, STEPS - 1, rows, part), bf16),
            pltpu.VMEM((2, STEPS, holders, rows, part), bf16),
            pltpu.VMEM((2, STEPS, 2, chips, rows, part), bf16),
            pltpu.VMEM((2, STEPS, chips, rows, part), bf16),
            pltpu.VMEM((2, STEPS, chips, rows, part), bf16),
            pltpu.VMEM((2, STEPS, chips - 1, rows, part), bf16),
            pltpu.VMEM((2, STEPS, rows, part), bf16),
            pltpu.VMEM((2, STEPS, STEPS, rows, part), bf16),
            pltpu.VMEM((2, tokens, width), bf16),
            dma((3,)),
            dma((3,)),
            dma((3,)),
            dma((2, STEPS - 1)),
            dma((2, STEPS - 1)),
            dma((2, STEPS, holders)),
            dma((2, STEPS, holders)),
            dma((2, STEPS)),
            dma((2, STEPS)),
            dma((2, STEPS, chips - 1)),
            dma((2, STEPS, chips - 1)),
            dma((2, STEPS, STEPS)),
            dma((2, STEPS, STEPS)),
            dma((2, CHUNKS)),
            dma((2, CHUNKS)),
        ],
        compiler_params=pltpu.CompilerParams(
            collective_id=0, has_side_effects=True, vmem_limit_bytes=48 * 1024 * 1024
        ),
        cost_estimate=pl.CostEstimate(
            flops=1_000_000_000, bytes_accessed=8_000_000, transcendentals=100_000
        ),
    )(fwd_state, rev_state, norm_gain, routes, scores, w_gate, w_up, w_down)


def solution(mesh):
    in_specs = (
        P("pipe", "expert", None),
        P("pipe", "expert", None),
        P("pipe", None),
        P("pipe", None, "expert"),
        P("pipe", None, "expert"),
        P("pipe", "expert", None),
        P(None, "pipe", "expert", None),
        P(None, "pipe", "expert", None),
        P(None, "pipe", "expert", None),
        P(None, "pipe", "expert", None),
    )
    out_specs = (P("pipe", "expert", None), P("pipe", "expert", None))
    small = mesh.shape["pipe"] == 4 and mesh.shape["expert"] == SPLIT
    local = relay_local if small else general_local
    return jax.shard_map(local, mesh=mesh, in_specs=in_specs, out_specs=out_specs, check_vma=False)
```

```python
import jax
import jax.numpy as jnp
from jax import lax
from jax.experimental import pallas as pl
from jax.experimental.pallas import tpu as pltpu
from jax.sharding import PartitionSpec as P

SPLIT = 8
CAP = 4
STEPS = 3
PARTS = 4
CHUNKS = 4

EPSILON = 1e-06
ROUTE_SCALE = 2.5
MESH = pl.DeviceIdType.MESH


def shifted(value, axis, steps):
    count = lax.axis_size(axis)
    pairs = [(source, (source + steps) % count) for source in range(count)]
    return lax.ppermute(value, axis, pairs)


def normalize(tok_rows, gain_row):
    values = tok_rows.astype(jnp.float32)
    factor = lax.rsqrt(jnp.mean(values * values, axis=-1, keepdims=True) + EPSILON)
    return (values * factor * gain_row).astype(jnp.bfloat16)


def slot_tables(route_ids, route_scores, flying):
    expert_ids = jnp.arange(flying, dtype=jnp.int32)
    matches = (route_ids[:, :, None] == expert_ids[None, None, :]).astype(jnp.float32)
    hit_mask = jnp.sum(matches, axis=1)
    weighted = (
        ROUTE_SCALE
        * jnp.sum(matches * route_scores[:, :, None], axis=1)
        / jnp.sum(route_scores, axis=1, keepdims=True)
    )
    slot_index = jnp.cumsum(hit_mask, axis=0) - 1.0
    slot_ids = jnp.arange(CAP, dtype=jnp.float32)
    placed = hit_mask.T[:, None, :] * (slot_index.T[:, None, :] == slot_ids[None, :, None]).astype(
        jnp.float32
    )
    mix_table = placed * weighted.T[:, None, :]
    return (placed, mix_table)


def dispatch_slots(normed, placed):
    return jnp.einsum(
        "ecr,rd->ecd", placed, normed.astype(jnp.float32), precision=lax.Precision.HIGHEST
    ).astype(jnp.bfloat16)


def finish(tok_rows, summed, mix_table):
    added = jnp.einsum("ecr,ecd->rd", mix_table, summed, precision=lax.Precision.HIGHEST)
    return (tok_rows.astype(jnp.float32) + added).astype(jnp.bfloat16)


def general_local(
    fwd_state,
    rev_state,
    norm_gain,
    w_gate,
    w_up,
    w_down,
    routes_fwd,
    scores_fwd,
    routes_rev,
    scores_rev,
):
    flying = lax.axis_size("expert") // SPLIT
    width = fwd_state.shape[2]
    gain_row = norm_gain[0]
    gate_cols = w_gate[0]
    up_cols = w_up[0]
    down_rows = w_down[0]

    def prepare(current, route_ids, route_scores):
        normed = normalize(current[0], gain_row)
        placed, mix_table = slot_tables(route_ids, route_scores, flying)
        slot_rows = dispatch_slots(normed, placed)
        copies = jnp.broadcast_to(slot_rows[:, None], (flying, SPLIT, CAP, width)).reshape(
            flying * SPLIT, CAP, width
        )
        return (copies, mix_table)

    def finish_stream(current, returned, mix_table):
        summed = jnp.sum(returned.astype(jnp.float32).reshape(flying, SPLIT, CAP, width), axis=1)
        return finish(current[0], summed, mix_table)[None]

    forward_now = fwd_state
    reverse_now = rev_state
    for step_index in range(STEPS):
        fwd_copies, fwd_mix = prepare(
            forward_now, routes_fwd[step_index, 0], scores_fwd[step_index, 0]
        )
        rev_copies, rev_mix = prepare(
            reverse_now, routes_rev[step_index, 0], scores_rev[step_index, 0]
        )
        joined = jnp.concatenate([fwd_copies, rev_copies], axis=1)
        received = lax.all_to_all(joined, "expert", split_axis=0, concat_axis=0, tiled=True)
        tok_rows = received.reshape(-1, width)
        gate_act = jnp.dot(tok_rows, gate_cols, preferred_element_type=jnp.float32)
        up_act = jnp.dot(tok_rows, up_cols, preferred_element_type=jnp.float32)
        hidden = (jax.nn.silu(gate_act) * up_act).astype(jnp.bfloat16)
        partial_out = jnp.dot(hidden, down_rows, preferred_element_type=jnp.float32).astype(
            jnp.bfloat16
        )
        returned = lax.all_to_all(
            partial_out.reshape(received.shape), "expert", split_axis=0, concat_axis=0, tiled=True
        )
        fwd_back = returned[:, :CAP]
        rev_back = returned[:, CAP:]
        forward_now = shifted(finish_stream(forward_now, fwd_back, fwd_mix), "pipe", 1)
        reverse_now = shifted(finish_stream(reverse_now, rev_back, rev_mix), "pipe", -1)
    return (forward_now, reverse_now)


def relay_kernel(
    fwd_hbm,
    rev_hbm,
    gain_hbm,
    gate_hbm,
    up_hbm,
    down_hbm,
    routes_fwd_hbm,
    scores_fwd_hbm,
    routes_rev_hbm,
    scores_rev_hbm,
    fwd_out,
    rev_out,
    states,
    gain_ref,
    route_ref,
    score_ref,
    gate_up,
    down,
    table,
    table_in,
    early_out,
    early_in,
    slots,
    pieces,
    mate_pieces,
    chip_sums,
    returned,
    changed,
    changed_in,
    bulk_in,
    load_sem,
    table_send,
    table_recv,
    early_send,
    early_recv,
    slot_send,
    slot_recv,
    piece_send,
    piece_recv,
    back_send,
    back_recv,
    changed_send,
    changed_recv,
    bulk_send,
    bulk_recv,
):
    f32, bf16 = jnp.float32, jnp.bfloat16
    tokens, width = fwd_hbm.shape[1], fwd_hbm.shape[2]
    part = width // PARTS
    rows = PARTS * CAP
    sections = lax.axis_size("pipe")
    holders = lax.axis_size("expert")
    me_pipe = lax.axis_index("pipe")
    me_expert = lax.axis_index("expert")
    chips = holders // 2
    core = lax.rem(me_expert, 2)
    chip = me_expert // 2

    def at_section(offset):
        return {"pipe": lax.rem(me_pipe + sections + offset, sections)}

    def at_chip(offset):
        return {"expert": lax.rem(chip + chips + offset, chips) * 2 + core}

    mate = {"expert": chip * 2 + 1 - core}

    unsent = []

    def remote(source, target, send, recv, device):
        return pltpu.make_async_remote_copy(
            src_ref=source,
            dst_ref=target,
            send_sem=send,
            recv_sem=recv,
            device_id=device,
            device_id_type=MESH,
        )

    def launch(copy):
        copy.start()
        unsent.append(copy)

    barrier = pltpu.get_barrier_semaphore()
    peers = [at_section(d) for d in range(1, 4)] + [at_chip(k) for k in range(1, chips)] + [mate]
    for peer in peers:
        pl.semaphore_signal(barrier, inc=1, device_id=peer, device_id_type=MESH)

    loads = [
        (routes_fwd_hbm.at[:, 0], route_ref.at[0]),
        (routes_rev_hbm.at[:, 0], route_ref.at[1]),
        (scores_fwd_hbm.at[:, 0], score_ref.at[0]),
        (scores_rev_hbm.at[:, 0], score_ref.at[1]),
        (fwd_hbm.at[0], states.at[0]),
        (rev_hbm.at[0], states.at[1]),
        (gain_hbm, gain_ref),
        (gate_hbm.at[0], gate_up.at[:, 0:128]),
        (up_hbm.at[0], gate_up.at[:, 128:256]),
        (down_hbm.at[0], down),
    ]
    loads = [
        pltpu.make_async_copy(source, target, load_sem.at[i])
        for i, (source, target) in enumerate(loads)
    ]
    for copy in loads:
        copy.start()
    for copy in loads[:4]:
        copy.wait()

    before = (
        lax.broadcasted_iota(jnp.int32, (tokens, tokens), 0)
        <= lax.broadcasted_iota(jnp.int32, (tokens, tokens), 1)
    ).astype(f32)
    slot_of_row = lax.rem(lax.broadcasted_iota(jnp.int32, (8, tokens), 0), CAP).astype(f32)
    mix = {}
    for stream in range(2):
        for step in range(STEPS):
            match = (route_ref[stream, step] == 0).astype(f32)
            score = score_ref[stream, step]
            hit = jnp.sum(match, axis=0, keepdims=True)
            weighted = (
                ROUTE_SCALE
                * jnp.sum(match * score, axis=0, keepdims=True)
                / jnp.sum(score, axis=0, keepdims=True)
            )
            hits = jnp.broadcast_to(hit, (8, tokens))
            place = jnp.dot(hits, before, preferred_element_type=f32) - 1.0
            placed = hits * (place == slot_of_row).astype(f32)
            table[stream, step] = placed
            column = jnp.sum(placed * weighted, axis=1, keepdims=True)
            mix[stream, step] = jnp.concatenate([column, column], axis=0)

    part_of_row = lax.broadcasted_iota(jnp.int32, (rows, part), 0) // CAP

    def by_part(pick):
        total = pick(PARTS - 1)
        for q in range(PARTS - 1):
            total = jnp.where(part_of_row == q, pick(q), total)
        return total

    def cols(q):
        return slice(q * part, (q + 1) * part)

    def twice(placed):
        return jnp.concatenate([placed, placed], axis=0)

    def select(placed, state):
        marks = twice(placed).astype(bf16)
        return by_part(
            lambda q: jnp.dot(marks, state[:, cols(q)], preferred_element_type=f32)
        )

    for copy in loads[4:7]:
        copy.wait()
    gain = by_part(lambda q: jnp.broadcast_to(gain_ref[:, cols(q)], (rows, part)))

    def table_copy(d):
        return remote(
            table, table_in.at[d - 1], table_send.at[d - 1], table_recv.at[d - 1], at_section(d)
        )

    def sign(stream):
        return 1 if stream == 0 else -1

    def table_from(stream, behind):
        offset = behind if stream == 0 else (-behind) % 4
        return table_in.at[offset - 1, stream]

    def early_copy(stream, d):
        return remote(
            early_out.at[stream, d - 1],
            early_in.at[stream, d - 1],
            early_send.at[stream, d - 1],
            early_recv.at[stream, d - 1],
            at_section(sign(stream) * d),
        )

    def bulk_copy(stream, chunk):
        size = tokens // CHUNKS
        piece = pl.ds(chunk * size, size)
        return remote(
            states.at[stream, piece],
            bulk_in.at[stream, piece],
            bulk_send.at[stream, chunk],
            bulk_recv.at[stream, chunk],
            at_section(sign(stream) * 3),
        )

    def changed_copy(stream, step, d):
        return remote(
            changed.at[stream, step],
            changed_in.at[stream, step, d - 1],
            changed_send.at[stream, step, d - 1],
            changed_recv.at[stream, step, d - 1],
            at_section(sign(stream) * d),
        )

    def slot_copy(stream, step, k):
        return remote(
            slots.at[stream, step, 0],
            slots.at[stream, step, k],
            slot_send.at[stream, step, k],
            slot_recv.at[stream, step, k],
            at_chip(k),
        )

    def mate_copy(stream, step, k):
        return remote(
            slots.at[stream, step, k],
            slots.at[stream, step, chips + k],
            slot_send.at[stream, step, chips + k],
            slot_recv.at[stream, step, chips + k],
            mate,
        )

    def piece_copy(stream, step):
        return remote(
            pieces.at[stream, step, 1],
            mate_pieces.at[stream, step],
            piece_send.at[stream, step],
            piece_recv.at[stream, step],
            mate,
        )

    def back_copy(stream, step, k):
        return remote(
            chip_sums.at[stream, step, k],
            returned.at[stream, step, k - 1],
            back_send.at[stream, step, k - 1],
            back_recv.at[stream, step, k - 1],
            at_chip(-k),
        )

    row_part = lax.broadcasted_iota(jnp.int32, (rows, rows), 0) // CAP
    col_part = lax.broadcasted_iota(jnp.int32, (rows, rows), 1) // CAP
    same_part = (row_part == col_part).astype(f32)

    def chain(stream):
        for step in range(STEPS):
            own = table[stream, step]
            if step == 0:
                current = select(own, states.at[stream])
            else:
                early_copy(stream, step).wait_recv()
                current = early_in[stream, step - 1].astype(f32)
                for past in range(step):
                    behind = step - past
                    match = same_part * lax.dot_general(
                        twice(own),
                        twice(table_from(stream, behind)[past]),
                        (((1,), (1,)), ((), ())),
                        preferred_element_type=f32,
                    )
                    seen = jnp.sum(match, axis=1, keepdims=True)
                    changed_copy(stream, past, behind).wait_recv()
                    newer = jnp.dot(
                        match.astype(bf16),
                        changed_in[stream, past, behind - 1],
                        preferred_element_type=f32,
                    )
                    current = jnp.where(seen > 0.5, newer, current)
            squares = jnp.sum(current * current, axis=1, keepdims=True)
            squares = jnp.broadcast_to(squares, (rows, 128))
            squares = squares[:8] + squares[8:]
            squares = squares + pltpu.roll(squares, 4, 0)
            factor = lax.rsqrt(squares[:, :1] * (1.0 / width) + EPSILON)
            slots[stream, step, 0] = (current * twice(factor) * gain).astype(bf16)
            if step == 0 and stream == 0:
                pl.semaphore_wait(barrier, len(peers))
                tables_out()
            for k in (2, 1, 3):
                launch(slot_copy(stream, step, k))
            launch(mate_copy(stream, step, 0))
            yield
            for k in (1, 3, 2):
                slot_copy(stream, step, k).wait_recv()
                launch(mate_copy(stream, step, k))
            yield
            for k in range(chips):
                mate_copy(stream, step, k).wait_recv()
            if step == 0 and stream == 0:
                for copy in loads[7:]:
                    copy.wait()
            gathered = slots[stream, step].reshape(holders * rows, part)
            total = None
            part_of_line = (
                lax.broadcasted_iota(jnp.int32, (holders * rows, 256), 0) % rows
            ) // CAP
            for q in range(PARTS):
                product = jnp.dot(gathered, gate_up[cols(q), :], preferred_element_type=f32)
                total = product if q == 0 else jnp.where(part_of_line == q, product, total)
            total = total.reshape(holders, 2, 8, 256)
            total = total[:, 0] + total[:, 1]
            total = (total + pltpu.roll(total, 4, 1)).reshape(holders * 8, 256)
            gate_act, up_act = total[:, :128], total[:, 128:]
            hidden = (gate_act / (1.0 + jnp.exp(-gate_act)) * up_act).astype(bf16)
            low = lax.broadcasted_iota(jnp.int32, (holders * 8, part), 0) % 8 < CAP
            halves = []
            for half in range(2):
                one = jnp.dot(hidden, down[:, cols(2 * half)], preferred_element_type=f32)
                two = jnp.dot(hidden, down[:, cols(2 * half + 1)], preferred_element_type=f32)
                halves.append(jnp.where(low, one, two).reshape(holders, 1, 8, part))
            joined = jnp.concatenate(halves, axis=1).reshape(2, chips, rows, part)
            pieces[stream, step] = joined.astype(bf16)
            launch(piece_copy(stream, step))
            yield
            piece_copy(stream, step).wait_recv()
            sums = pieces[stream, step, 0].astype(f32) + mate_pieces[stream, step].astype(f32)
            chip_sums[stream, step] = sums.astype(bf16)
            for k in (2, 1, 3):
                launch(back_copy(stream, step, k))
            yield
            expert_out = sums[0]
            for k in range(1, chips):
                back_copy(stream, step, k).wait_recv()
                expert_out = expert_out + returned[stream, step, k - 1].astype(f32)
            changed[stream, step] = (current + mix[stream, step] * expert_out).astype(bf16)
            launch(changed_copy(stream, step, 1))
            yield
            farther.extend((stream, step, d) for d in range(2, STEPS - step + 1))

    def tables_out():
        for d in range(1, 4):
            launch(table_copy(d))

    def early_rows():
        for d in range(1, 4):
            table_copy(d).wait_recv()
        for stream in range(2):
            for d in range(1, STEPS):
                ahead = table_from(stream, 4 - d)
                early_out[stream, d - 1] = select(ahead[d], states.at[stream]).astype(bf16)
                launch(early_copy(stream, d))

    def bulk():
        for chunk in range(CHUNKS):
            for stream in range(2):
                launch(bulk_copy(stream, chunk))

    farther = []
    chains = [chain(0), chain(1)]
    second = chains[1]
    next(chains[0])
    turn = 0
    while chains:
        for one in list(chains):
            try:
                next(one)
            except StopIteration:
                chains.remove(one)
            if one is second:
                for stream, step, d in farther:
                    launch(changed_copy(stream, step, d))
                farther.clear()
        if turn == 0:
            early_rows()
            bulk()
        turn += 1

    lanes = 128
    slot_lane = lax.broadcasted_iota(jnp.int32, (tokens, lanes), 1)
    for stream, out in ((0, fwd_out), (1, rev_out)):
        marks = []
        for step in range(STEPS):
            placed = table_from(stream, STEPS - step)[step]
            for later in range(step + 1, STEPS):
                newer = table_from(stream, STEPS - later)[later]
                placed = placed * (1.0 - jnp.sum(newer[:CAP], axis=0, keepdims=True))
            marks.append(twice(placed))
        marks.append(jnp.zeros((lanes - STEPS * rows, tokens), f32))
        spread = jnp.concatenate(marks, axis=0).T
        seen = jnp.sum(spread, axis=1, keepdims=True) > 0.5
        for chunk in range(CHUNKS):
            bulk_copy(stream, chunk).wait_recv()
        for step in range(STEPS):
            changed_copy(stream, step, STEPS - step).wait_recv()
        newest = [changed_in[stream, step, STEPS - step - 1] for step in range(STEPS)]
        newest.append(jnp.zeros((lanes - STEPS * rows, part), bf16))
        newest = jnp.concatenate(newest, axis=0)
        for q in range(PARTS):
            chosen = jnp.where(lax.rem(slot_lane, rows) // CAP == q, spread, 0.0).astype(bf16)
            newer = jnp.dot(chosen, newest, preferred_element_type=f32)
            older = bulk_in[stream, :, cols(q)].astype(f32)
            out[0, :, cols(q)] = jnp.where(seen, newer, older).astype(bf16)

    for copy in unsent:
        copy.wait_send()


def relay_local(
    fwd_state,
    rev_state,
    norm_gain,
    w_gate,
    w_up,
    w_down,
    routes_fwd,
    scores_fwd,
    routes_rev,
    scores_rev,
):
    tokens, width = fwd_state.shape[1:]
    part = width // PARTS
    rows = PARTS * CAP
    holders = SPLIT
    chips = holders // 2
    bf16 = jnp.bfloat16

    in_hbm = pl.BlockSpec(memory_space=pltpu.HBM)
    vmem = pl.BlockSpec(memory_space=pltpu.VMEM)
    names = routes_fwd.shape[3]
    dma = pltpu.SemaphoreType.DMA
    return pl.pallas_call(
        relay_kernel,
        out_shape=[jax.ShapeDtypeStruct(fwd_state.shape, bf16)] * 2,
        in_specs=[in_hbm] * 10,
        out_specs=[vmem, vmem],
        scratch_shapes=[
            pltpu.VMEM((2, tokens, width), bf16),
            pltpu.VMEM((1, width), jnp.float32),
            pltpu.VMEM((2, STEPS, names, tokens), jnp.int32),
            pltpu.VMEM((2, STEPS, names, tokens), jnp.float32),
            pltpu.VMEM((width, 256), bf16),
            pltpu.VMEM((128, width), bf16),
            pltpu.VMEM((2, STEPS, 8, tokens), jnp.float32),
            pltpu.VMEM((3, 2, STEPS, 8, tokens), jnp.float32),
            pltpu.VMEM((2, STEPS - 1, rows, part), bf16),
            pltpu.VMEM((2, STEPS - 1, rows, part), bf16),
            pltpu.VMEM((2, STEPS, holders, rows, part), bf16),
            pltpu.VMEM((2, STEPS, 2, chips, rows, part), bf16),
            pltpu.VMEM((2, STEPS, chips, rows, part), bf16),
            pltpu.VMEM((2, STEPS, chips, rows, part), bf16),
            pltpu.VMEM((2, STEPS, chips - 1, rows, part), bf16),
            pltpu.VMEM((2, STEPS, rows, part), bf16),
            pltpu.VMEM((2, STEPS, STEPS, rows, part), bf16),
            pltpu.VMEM((2, tokens, width), bf16),
            dma((10,)),
            dma((3,)),
            dma((3,)),
            dma((2, STEPS - 1)),
            dma((2, STEPS - 1)),
            dma((2, STEPS, holders)),
            dma((2, STEPS, holders)),
            dma((2, STEPS)),
            dma((2, STEPS)),
            dma((2, STEPS, chips - 1)),
            dma((2, STEPS, chips - 1)),
            dma((2, STEPS, STEPS)),
            dma((2, STEPS, STEPS)),
            dma((2, CHUNKS)),
            dma((2, CHUNKS)),
        ],
        compiler_params=pltpu.CompilerParams(
            collective_id=0, has_side_effects=True, vmem_limit_bytes=64 * 1024 * 1024
        ),
        cost_estimate=pl.CostEstimate(
            flops=1_000_000_000, bytes_accessed=8_000_000, transcendentals=100_000
        ),
    )(
        fwd_state,
        rev_state,
        norm_gain,
        w_gate,
        w_up,
        w_down,
        *(x.transpose(0, 1, 3, 2) for x in (routes_fwd, scores_fwd, routes_rev, scores_rev)),
    )


def solution(mesh):
    in_specs = (
        P("pipe", "expert", None),
        P("pipe", "expert", None),
        P("pipe", None),
        P("pipe", None, "expert"),
        P("pipe", None, "expert"),
        P("pipe", "expert", None),
        P(None, "pipe", "expert", None),
        P(None, "pipe", "expert", None),
        P(None, "pipe", "expert", None),
        P(None, "pipe", "expert", None),
    )
    out_specs = (P("pipe", "expert", None), P("pipe", "expert", None))
    small = mesh.shape["pipe"] == 4 and mesh.shape["expert"] == SPLIT
    local = relay_local if small else general_local
    return jax.shard_map(local, mesh=mesh, in_specs=in_specs, out_specs=out_specs, check_vma=False)
```

```python
import jax
import jax.numpy as jnp
from jax import lax
from jax.experimental import pallas as pl
from jax.experimental.pallas import tpu as pltpu
from jax.sharding import PartitionSpec as P

SPLIT = 8
CAP = 4
STEPS = 3
PARTS = 4
CHUNKS = 4

EPSILON = 1e-06
ROUTE_SCALE = 2.5
MESH = pl.DeviceIdType.MESH


def shifted(value, axis, steps):
    count = lax.axis_size(axis)
    pairs = [(source, (source + steps) % count) for source in range(count)]
    return lax.ppermute(value, axis, pairs)


def normalize(tok_rows, gain_row):
    values = tok_rows.astype(jnp.float32)
    factor = lax.rsqrt(jnp.mean(values * values, axis=-1, keepdims=True) + EPSILON)
    return (values * factor * gain_row).astype(jnp.bfloat16)


def slot_tables(route_ids, route_scores, flying):
    expert_ids = jnp.arange(flying, dtype=jnp.int32)
    matches = (route_ids[:, :, None] == expert_ids[None, None, :]).astype(jnp.float32)
    hit_mask = jnp.sum(matches, axis=1)
    weighted = (
        ROUTE_SCALE
        * jnp.sum(matches * route_scores[:, :, None], axis=1)
        / jnp.sum(route_scores, axis=1, keepdims=True)
    )
    slot_index = jnp.cumsum(hit_mask, axis=0) - 1.0
    slot_ids = jnp.arange(CAP, dtype=jnp.float32)
    placed = hit_mask.T[:, None, :] * (slot_index.T[:, None, :] == slot_ids[None, :, None]).astype(
        jnp.float32
    )
    mix_table = placed * weighted.T[:, None, :]
    return (placed, mix_table)


def dispatch_slots(normed, placed):
    return jnp.einsum(
        "ecr,rd->ecd", placed, normed.astype(jnp.float32), precision=lax.Precision.HIGHEST
    ).astype(jnp.bfloat16)


def finish(tok_rows, summed, mix_table):
    added = jnp.einsum("ecr,ecd->rd", mix_table, summed, precision=lax.Precision.HIGHEST)
    return (tok_rows.astype(jnp.float32) + added).astype(jnp.bfloat16)


def general_local(
    fwd_state,
    rev_state,
    norm_gain,
    w_gate,
    w_up,
    w_down,
    routes_fwd,
    scores_fwd,
    routes_rev,
    scores_rev,
):
    flying = lax.axis_size("expert") // SPLIT
    width = fwd_state.shape[2]
    gain_row = norm_gain[0]
    gate_cols = w_gate[0]
    up_cols = w_up[0]
    down_rows = w_down[0]

    def prepare(current, route_ids, route_scores):
        normed = normalize(current[0], gain_row)
        placed, mix_table = slot_tables(route_ids, route_scores, flying)
        slot_rows = dispatch_slots(normed, placed)
        copies = jnp.broadcast_to(slot_rows[:, None], (flying, SPLIT, CAP, width)).reshape(
            flying * SPLIT, CAP, width
        )
        return (copies, mix_table)

    def finish_stream(current, returned, mix_table):
        summed = jnp.sum(returned.astype(jnp.float32).reshape(flying, SPLIT, CAP, width), axis=1)
        return finish(current[0], summed, mix_table)[None]

    forward_now = fwd_state
    reverse_now = rev_state
    for step_index in range(STEPS):
        fwd_copies, fwd_mix = prepare(
            forward_now, routes_fwd[step_index, 0], scores_fwd[step_index, 0]
        )
        rev_copies, rev_mix = prepare(
            reverse_now, routes_rev[step_index, 0], scores_rev[step_index, 0]
        )
        joined = jnp.concatenate([fwd_copies, rev_copies], axis=1)
        received = lax.all_to_all(joined, "expert", split_axis=0, concat_axis=0, tiled=True)
        tok_rows = received.reshape(-1, width)
        gate_act = jnp.dot(tok_rows, gate_cols, preferred_element_type=jnp.float32)
        up_act = jnp.dot(tok_rows, up_cols, preferred_element_type=jnp.float32)
        hidden = (jax.nn.silu(gate_act) * up_act).astype(jnp.bfloat16)
        partial_out = jnp.dot(hidden, down_rows, preferred_element_type=jnp.float32).astype(
            jnp.bfloat16
        )
        returned = lax.all_to_all(
            partial_out.reshape(received.shape), "expert", split_axis=0, concat_axis=0, tiled=True
        )
        fwd_back = returned[:, :CAP]
        rev_back = returned[:, CAP:]
        forward_now = shifted(finish_stream(forward_now, fwd_back, fwd_mix), "pipe", 1)
        reverse_now = shifted(finish_stream(reverse_now, rev_back, rev_mix), "pipe", -1)
    return (forward_now, reverse_now)


def relay_kernel(
    fwd_hbm,
    rev_hbm,
    gain_hbm,
    gate_hbm,
    up_hbm,
    down_hbm,
    routes_fwd_hbm,
    scores_fwd_hbm,
    routes_rev_hbm,
    scores_rev_hbm,
    fwd_out,
    rev_out,
    states,
    gain_ref,
    route_ref,
    score_ref,
    gate_up,
    down,
    table,
    table_in,
    early_out,
    early_in,
    slots,
    pieces,
    mate_pieces,
    chip_sums,
    returned,
    changed,
    changed_in,
    bulk_in,
    load_sem,
    table_send,
    table_recv,
    early_send,
    early_recv,
    slot_send,
    mate_send,
    slot_recv,
    piece_send,
    piece_recv,
    back_send,
    back_recv,
    changed_send,
    changed_recv,
    bulk_send,
    bulk_recv,
):
    f32, bf16 = jnp.float32, jnp.bfloat16
    tokens, width = fwd_hbm.shape[1], fwd_hbm.shape[2]
    part = width // PARTS
    rows = PARTS * CAP
    sections = lax.axis_size("pipe")
    holders = lax.axis_size("expert")
    me_pipe = lax.axis_index("pipe")
    me_expert = lax.axis_index("expert")
    chips = holders // 2
    core = lax.rem(me_expert, 2)
    chip = me_expert // 2

    def at_section(offset):
        return {"pipe": lax.rem(me_pipe + sections + offset, sections)}

    def at_chip(offset):
        return {"expert": lax.rem(chip + chips + offset, chips) * 2 + core}

    mate = {"expert": chip * 2 + 1 - core}

    unsent = []

    def remote(source, target, send, recv, device):
        return pltpu.make_async_remote_copy(
            src_ref=source,
            dst_ref=target,
            send_sem=send,
            recv_sem=recv,
            device_id=device,
            device_id_type=MESH,
        )

    def launch(copy, only=None):
        if only is None:
            copy.start()
        else:
            pl.when(only)(copy.start)
        unsent.append((copy, only))

    returned[...] = jnp.zeros_like(returned)
    barrier = pltpu.get_barrier_semaphore()
    peers = [at_section(d) for d in range(1, 4)] + [at_chip(k) for k in range(1, chips)] + [mate]
    for peer in peers:
        pl.semaphore_signal(barrier, inc=1, device_id=peer, device_id_type=MESH)

    loads = [
        (routes_fwd_hbm.at[:, 0], route_ref.at[0]),
        (routes_rev_hbm.at[:, 0], route_ref.at[1]),
        (scores_fwd_hbm.at[:, 0], score_ref.at[0]),
        (scores_rev_hbm.at[:, 0], score_ref.at[1]),
        (fwd_hbm.at[0], states.at[0]),
        (rev_hbm.at[0], states.at[1]),
        (gain_hbm, gain_ref),
        (gate_hbm.at[0], gate_up.at[:, 0:128]),
        (up_hbm.at[0], gate_up.at[:, 128:256]),
        (down_hbm.at[0], down),
    ]
    loads = [
        pltpu.make_async_copy(source, target, load_sem.at[i])
        for i, (source, target) in enumerate(loads)
    ]
    for copy in loads:
        copy.start()
    for copy in loads[:4]:
        copy.wait()

    before = (
        lax.broadcasted_iota(jnp.int32, (tokens, tokens), 0)
        <= lax.broadcasted_iota(jnp.int32, (tokens, tokens), 1)
    ).astype(f32)
    slot_of_row = lax.rem(lax.broadcasted_iota(jnp.int32, (8, tokens), 0), CAP).astype(f32)
    mix = {}
    for stream in range(2):
        for step in range(STEPS):
            match = (route_ref[stream, step] == 0).astype(f32)
            score = score_ref[stream, step]
            hit = jnp.sum(match, axis=0, keepdims=True)
            weighted = (
                ROUTE_SCALE
                * jnp.sum(match * score, axis=0, keepdims=True)
                / jnp.sum(score, axis=0, keepdims=True)
            )
            hits = jnp.broadcast_to(hit, (8, tokens))
            place = jnp.dot(hits, before, preferred_element_type=f32) - 1.0
            placed = hits * (place == slot_of_row).astype(f32)
            table[stream, step] = placed
            column = jnp.sum(placed * weighted, axis=1, keepdims=True)
            mix[stream, step] = jnp.concatenate([column, column], axis=0)

    part_of_row = lax.broadcasted_iota(jnp.int32, (rows, part), 0) // CAP

    def by_part(pick):
        total = pick(PARTS - 1)
        for q in range(PARTS - 1):
            total = jnp.where(part_of_row == q, pick(q), total)
        return total

    def cols(q):
        return slice(q * part, (q + 1) * part)

    def twice(placed):
        return jnp.concatenate([placed, placed], axis=0)

    def select(placed, state):
        marks = twice(placed).astype(bf16)
        return by_part(
            lambda q: jnp.dot(marks, state[:, cols(q)], preferred_element_type=f32)
        )

    for copy in loads[4:7]:
        copy.wait()
    gain = by_part(lambda q: jnp.broadcast_to(gain_ref[:, cols(q)], (rows, part)))

    def table_copy(d):
        return remote(
            table, table_in.at[d - 1], table_send.at[d - 1], table_recv.at[d - 1], at_section(d)
        )

    def sign(stream):
        return 1 if stream == 0 else -1

    def table_from(stream, behind):
        offset = behind if stream == 0 else (-behind) % 4
        return table_in.at[offset - 1, stream]

    def early_copy(stream, d):
        return remote(
            early_out.at[stream, d - 1],
            early_in.at[stream, d - 1],
            early_send.at[stream, d - 1],
            early_recv.at[stream, d - 1],
            at_section(sign(stream) * d),
        )

    def bulk_copy(stream, chunk):
        size = tokens // CHUNKS
        piece = pl.ds(chunk * size, size)
        return remote(
            states.at[stream, piece],
            bulk_in.at[stream, piece],
            bulk_send.at[stream, chunk],
            bulk_recv.at[stream, chunk],
            at_section(sign(stream) * 3),
        )

    def changed_copy(stream, step, d):
        return remote(
            changed.at[stream, step],
            changed_in.at[stream, step, d - 1],
            changed_send.at[stream, step, d - 1],
            changed_recv.at[stream, step, d - 1],
            at_section(sign(stream) * d),
        )

    last = chips - 1

    def slot_copy(stream, step, k, way):
        target = (k + way) % chips
        return remote(
            slots.at[stream, step, k],
            slots.at[stream, step, target],
            slot_send.at[stream, step, k, (way + 1) // 2],
            slot_recv.at[stream, step, target],
            at_chip(way),
        )

    def slot_arrives(stream, step, k):
        slot_copy(stream, step, k - 1, 1).wait_recv()

    def mate_copy(stream, step, k):
        return remote(
            slots.at[stream, step, k],
            slots.at[stream, step, chips + k],
            mate_send.at[stream, step, k],
            slot_recv.at[stream, step, chips + k],
            mate,
        )

    def piece_copy(stream, step):
        return remote(
            pieces.at[stream, step, 1],
            mate_pieces.at[stream, step],
            piece_send.at[stream, step],
            piece_recv.at[stream, step],
            mate,
        )

    def back_copy(stream, step, way, far):
        k = chips - far if way > 0 else far
        return remote(
            chip_sums.at[stream, step, k],
            returned.at[stream, step, (way + 1) // 2, far - 1],
            back_send.at[stream, step, k],
            back_recv.at[stream, step, (way + 1) // 2, far - 1],
            at_chip(way),
        )

    def back_arrives(stream, step, way, far):
        if way > 0:
            here = jnp.logical_and(chip >= 1, chip + far <= last)
        else:
            here = jnp.logical_and(chip < last, chip >= far)
        pl.when(here)(back_copy(stream, step, way, far + 1).wait_recv)

    def back_adds(stream, step, way, far):
        return returned[stream, step, (way + 1) // 2, far].astype(f32)

    row_part = lax.broadcasted_iota(jnp.int32, (rows, rows), 0) // CAP
    col_part = lax.broadcasted_iota(jnp.int32, (rows, rows), 1) // CAP
    same_part = (row_part == col_part).astype(f32)

    def chain(stream):
        for step in range(STEPS):
            own = table[stream, step]
            if step == 0:
                current = select(own, states.at[stream])
            else:
                early_copy(stream, step).wait_recv()
                current = early_in[stream, step - 1].astype(f32)
                for past in range(step):
                    behind = step - past
                    match = same_part * lax.dot_general(
                        twice(own),
                        twice(table_from(stream, behind)[past]),
                        (((1,), (1,)), ((), ())),
                        preferred_element_type=f32,
                    )
                    seen = jnp.sum(match, axis=1, keepdims=True)
                    changed_copy(stream, past, behind).wait_recv()
                    newer = jnp.dot(
                        match.astype(bf16),
                        changed_in[stream, past, behind - 1],
                        preferred_element_type=f32,
                    )
                    current = jnp.where(seen > 0.5, newer, current)
            squares = jnp.sum(current * current, axis=1, keepdims=True)
            squares = jnp.broadcast_to(squares, (rows, 128))
            squares = squares[:8] + squares[8:]
            squares = squares + pltpu.roll(squares, 4, 0)
            factor = lax.rsqrt(squares[:, :1] * (1.0 / width) + EPSILON)
            slots[stream, step, 0] = (current * twice(factor) * gain).astype(bf16)
            if step == 0 and stream == 0:
                pl.semaphore_wait(barrier, len(peers))
                tables_out()
            launch(slot_copy(stream, step, 0, 1), chip < last)
            launch(slot_copy(stream, step, 0, -1), chip > 0)
            launch(mate_copy(stream, step, 0))
            yield
            for k in (1, 3, 2):
                slot_arrives(stream, step, k)
                if k < last:
                    launch(
                        slot_copy(stream, step, k, 1), jnp.logical_and(chip >= k, chip < last)
                    )
                if k > 1:
                    launch(
                        slot_copy(stream, step, k, -1), jnp.logical_and(chip < k, chip > 0)
                    )
                launch(mate_copy(stream, step, k))
                if k != 1:
                    yield
            for k in range(chips):
                mate_copy(stream, step, k).wait_recv()
            if step == 0 and stream == 0:
                for copy in loads[7:]:
                    copy.wait()
            gathered = slots[stream, step].reshape(holders * rows, part)
            total = None
            part_of_line = (
                lax.broadcasted_iota(jnp.int32, (holders * rows, 256), 0) % rows
            ) // CAP
            for q in range(PARTS):
                product = jnp.dot(gathered, gate_up[cols(q), :], preferred_element_type=f32)
                total = product if q == 0 else jnp.where(part_of_line == q, product, total)
            total = total.reshape(holders, 2, 8, 256)
            total = total[:, 0] + total[:, 1]
            total = (total + pltpu.roll(total, 4, 1)).reshape(holders * 8, 256)
            gate_act, up_act = total[:, :128], total[:, 128:]
            hidden = (gate_act / (1.0 + jnp.exp(-gate_act)) * up_act).astype(bf16)
            low = lax.broadcasted_iota(jnp.int32, (holders * 8, part), 0) % 8 < CAP
            halves = []
            for half in range(2):
                one = jnp.dot(hidden, down[:, cols(2 * half)], preferred_element_type=f32)
                two = jnp.dot(hidden, down[:, cols(2 * half + 1)], preferred_element_type=f32)
                halves.append(jnp.where(low, one, two).reshape(holders, 1, 8, part))
            joined = jnp.concatenate(halves, axis=1).reshape(2, chips, rows, part)
            pieces[stream, step] = joined.astype(bf16)
            launch(piece_copy(stream, step))
            yield
            piece_copy(stream, step).wait_recv()
            sums = pieces[stream, step, 0].astype(f32) + mate_pieces[stream, step].astype(f32)

            def send_back(k, total, way, far, only):
                def store():
                    chip_sums[stream, step, k] = total.astype(bf16)

                pl.when(only)(store)
                launch(back_copy(stream, step, way, far), only)

            send_back(1, sums[1], 1, 3, chip == 0)
            send_back(3, sums[3], -1, 3, chip == last)
            yield
            back_arrives(stream, step, 1, 2)
            back_arrives(stream, step, -1, 2)
            both = sums[2] + back_adds(stream, step, 1, 2) + back_adds(stream, step, -1, 2)
            send_back(2, both, 1, 2, chip < 2)
            send_back(2, both, -1, 2, chip >= 2)
            yield
            back_arrives(stream, step, 1, 1)
            back_arrives(stream, step, -1, 1)
            send_back(3, sums[3] + back_adds(stream, step, 1, 1), 1, 1, chip < last)
            send_back(1, sums[1] + back_adds(stream, step, -1, 1), -1, 1, chip > 0)
            yield
            back_arrives(stream, step, 1, 0)
            back_arrives(stream, step, -1, 0)
            expert_out = sums[0] + back_adds(stream, step, 1, 0) + back_adds(stream, step, -1, 0)
            changed[stream, step] = (current + mix[stream, step] * expert_out).astype(bf16)
            launch(changed_copy(stream, step, 1))
            yield
            farther.extend((stream, step, d) for d in range(2, STEPS - step + 1))

    def tables_out():
        for d in range(1, 4):
            launch(table_copy(d))

    def early_rows():
        for d in range(1, 4):
            table_copy(d).wait_recv()
        for stream in range(2):
            for d in range(1, STEPS):
                ahead = table_from(stream, 4 - d)
                early_out[stream, d - 1] = select(ahead[d], states.at[stream]).astype(bf16)
                launch(early_copy(stream, d))

    def bulk():
        for chunk in range(CHUNKS):
            for stream in range(2):
                launch(bulk_copy(stream, chunk))

    farther = []
    chains = [chain(0), chain(1)]
    second = chains[1]
    turn = 0
    while chains:
        for one in list(chains):
            try:
                next(one)
            except StopIteration:
                chains.remove(one)
            if one is second:
                for stream, step, d in farther:
                    launch(changed_copy(stream, step, d))
                farther.clear()
        if turn == 1:
            early_rows()
            bulk()
        turn += 1

    lanes = 128
    slot_lane = lax.broadcasted_iota(jnp.int32, (tokens, lanes), 1)
    for stream, out in ((0, fwd_out), (1, rev_out)):
        marks = []
        for step in range(STEPS):
            placed = table_from(stream, STEPS - step)[step]
            for later in range(step + 1, STEPS):
                newer = table_from(stream, STEPS - later)[later]
                placed = placed * (1.0 - jnp.sum(newer[:CAP], axis=0, keepdims=True))
            marks.append(twice(placed))
        marks.append(jnp.zeros((lanes - STEPS * rows, tokens), f32))
        spread = jnp.concatenate(marks, axis=0).T
        seen = jnp.sum(spread, axis=1, keepdims=True) > 0.5
        for chunk in range(CHUNKS):
            bulk_copy(stream, chunk).wait_recv()
        for step in range(STEPS):
            changed_copy(stream, step, STEPS - step).wait_recv()
        newest = [changed_in[stream, step, STEPS - step - 1] for step in range(STEPS)]
        newest.append(jnp.zeros((lanes - STEPS * rows, part), bf16))
        newest = jnp.concatenate(newest, axis=0)
        for q in range(PARTS):
            chosen = jnp.where(lax.rem(slot_lane, rows) // CAP == q, spread, 0.0).astype(bf16)
            newer = jnp.dot(chosen, newest, preferred_element_type=f32)
            older = bulk_in[stream, :, cols(q)].astype(f32)
            out[0, :, cols(q)] = jnp.where(seen, newer, older).astype(bf16)

    for copy, only in unsent:
        if only is None:
            copy.wait_send()
        else:
            pl.when(only)(copy.wait_send)


def relay_local(
    fwd_state,
    rev_state,
    norm_gain,
    w_gate,
    w_up,
    w_down,
    routes_fwd,
    scores_fwd,
    routes_rev,
    scores_rev,
):
    tokens, width = fwd_state.shape[1:]
    part = width // PARTS
    rows = PARTS * CAP
    holders = SPLIT
    chips = holders // 2
    bf16 = jnp.bfloat16

    in_hbm = pl.BlockSpec(memory_space=pltpu.HBM)
    vmem = pl.BlockSpec(memory_space=pltpu.VMEM)
    names = routes_fwd.shape[3]
    dma = pltpu.SemaphoreType.DMA
    return pl.pallas_call(
        relay_kernel,
        out_shape=[jax.ShapeDtypeStruct(fwd_state.shape, bf16)] * 2,
        in_specs=[in_hbm] * 10,
        out_specs=[vmem, vmem],
        scratch_shapes=[
            pltpu.VMEM((2, tokens, width), bf16),
            pltpu.VMEM((1, width), jnp.float32),
            pltpu.VMEM((2, STEPS, names, tokens), jnp.int32),
            pltpu.VMEM((2, STEPS, names, tokens), jnp.float32),
            pltpu.VMEM((width, 256), bf16),
            pltpu.VMEM((128, width), bf16),
            pltpu.VMEM((2, STEPS, 8, tokens), jnp.float32),
            pltpu.VMEM((3, 2, STEPS, 8, tokens), jnp.float32),
            pltpu.VMEM((2, STEPS - 1, rows, part), bf16),
            pltpu.VMEM((2, STEPS - 1, rows, part), bf16),
            pltpu.VMEM((2, STEPS, holders, rows, part), bf16),
            pltpu.VMEM((2, STEPS, 2, chips, rows, part), bf16),
            pltpu.VMEM((2, STEPS, chips, rows, part), bf16),
            pltpu.VMEM((2, STEPS, chips, rows, part), bf16),
            pltpu.VMEM((2, STEPS, 2, chips - 1, rows, part), bf16),
            pltpu.VMEM((2, STEPS, rows, part), bf16),
            pltpu.VMEM((2, STEPS, STEPS, rows, part), bf16),
            pltpu.VMEM((2, tokens, width), bf16),
            dma((10,)),
            dma((3,)),
            dma((3,)),
            dma((2, STEPS - 1)),
            dma((2, STEPS - 1)),
            dma((2, STEPS, chips, 2)),
            dma((2, STEPS, chips)),
            dma((2, STEPS, holders)),
            dma((2, STEPS)),
            dma((2, STEPS)),
            dma((2, STEPS, chips)),
            dma((2, STEPS, 2, chips - 1)),
            dma((2, STEPS, STEPS)),
            dma((2, STEPS, STEPS)),
            dma((2, CHUNKS)),
            dma((2, CHUNKS)),
        ],
        compiler_params=pltpu.CompilerParams(
            collective_id=0, has_side_effects=True, vmem_limit_bytes=64 * 1024 * 1024
        ),
        cost_estimate=pl.CostEstimate(
            flops=1_000_000_000, bytes_accessed=8_000_000, transcendentals=100_000
        ),
    )(
        fwd_state,
        rev_state,
        norm_gain,
        w_gate,
        w_up,
        w_down,
        *(x.transpose(0, 1, 3, 2) for x in (routes_fwd, scores_fwd, routes_rev, scores_rev)),
    )


def solution(mesh):
    in_specs = (
        P("pipe", "expert", None),
        P("pipe", "expert", None),
        P("pipe", None),
        P("pipe", None, "expert"),
        P("pipe", None, "expert"),
        P("pipe", "expert", None),
        P(None, "pipe", "expert", None),
        P(None, "pipe", "expert", None),
        P(None, "pipe", "expert", None),
        P(None, "pipe", "expert", None),
    )
    out_specs = (P("pipe", "expert", None), P("pipe", "expert", None))
    small = mesh.shape["pipe"] == 4 and mesh.shape["expert"] == SPLIT
    local = relay_local if small else general_local
    return jax.shard_map(local, mesh=mesh, in_specs=in_specs, out_specs=out_specs, check_vma=False)
```

```python
import jax
import jax.numpy as jnp
from jax import lax
from jax.experimental import pallas as pl
from jax.experimental.pallas import tpu as pltpu
from jax.sharding import PartitionSpec as P

SPLIT = 8
CAP = 4
STEPS = 3
PARTS = 4
CHUNKS = 16

EPSILON = 1e-06
ROUTE_SCALE = 2.5
MESH = pl.DeviceIdType.MESH


def shifted(value, axis, steps):
    count = lax.axis_size(axis)
    pairs = [(source, (source + steps) % count) for source in range(count)]
    return lax.ppermute(value, axis, pairs)


def normalize(tok_rows, gain_row):
    values = tok_rows.astype(jnp.float32)
    factor = lax.rsqrt(jnp.mean(values * values, axis=-1, keepdims=True) + EPSILON)
    return (values * factor * gain_row).astype(jnp.bfloat16)


def slot_tables(route_ids, route_scores, flying):
    expert_ids = jnp.arange(flying, dtype=jnp.int32)
    matches = (route_ids[:, :, None] == expert_ids[None, None, :]).astype(jnp.float32)
    hit_mask = jnp.sum(matches, axis=1)
    weighted = (
        ROUTE_SCALE
        * jnp.sum(matches * route_scores[:, :, None], axis=1)
        / jnp.sum(route_scores, axis=1, keepdims=True)
    )
    slot_index = jnp.cumsum(hit_mask, axis=0) - 1.0
    slot_ids = jnp.arange(CAP, dtype=jnp.float32)
    placed = hit_mask.T[:, None, :] * (slot_index.T[:, None, :] == slot_ids[None, :, None]).astype(
        jnp.float32
    )
    mix_table = placed * weighted.T[:, None, :]
    return (placed, mix_table)


def dispatch_slots(normed, placed):
    return jnp.einsum(
        "ecr,rd->ecd", placed, normed.astype(jnp.float32), precision=lax.Precision.HIGHEST
    ).astype(jnp.bfloat16)


def finish(tok_rows, summed, mix_table):
    added = jnp.einsum("ecr,ecd->rd", mix_table, summed, precision=lax.Precision.HIGHEST)
    return (tok_rows.astype(jnp.float32) + added).astype(jnp.bfloat16)


def general_local(
    fwd_state,
    rev_state,
    norm_gain,
    w_gate,
    w_up,
    w_down,
    routes_fwd,
    scores_fwd,
    routes_rev,
    scores_rev,
):
    flying = lax.axis_size("expert") // SPLIT
    width = fwd_state.shape[2]
    gain_row = norm_gain[0]
    gate_cols = w_gate[0]
    up_cols = w_up[0]
    down_rows = w_down[0]

    def prepare(current, route_ids, route_scores):
        normed = normalize(current[0], gain_row)
        placed, mix_table = slot_tables(route_ids, route_scores, flying)
        slot_rows = dispatch_slots(normed, placed)
        copies = jnp.broadcast_to(slot_rows[:, None], (flying, SPLIT, CAP, width)).reshape(
            flying * SPLIT, CAP, width
        )
        return (copies, mix_table)

    def finish_stream(current, returned, mix_table):
        summed = jnp.sum(returned.astype(jnp.float32).reshape(flying, SPLIT, CAP, width), axis=1)
        return finish(current[0], summed, mix_table)[None]

    forward_now = fwd_state
    reverse_now = rev_state
    for step_index in range(STEPS):
        fwd_copies, fwd_mix = prepare(
            forward_now, routes_fwd[step_index, 0], scores_fwd[step_index, 0]
        )
        rev_copies, rev_mix = prepare(
            reverse_now, routes_rev[step_index, 0], scores_rev[step_index, 0]
        )
        joined = jnp.concatenate([fwd_copies, rev_copies], axis=1)
        received = lax.all_to_all(joined, "expert", split_axis=0, concat_axis=0, tiled=True)
        tok_rows = received.reshape(-1, width)
        gate_act = jnp.dot(tok_rows, gate_cols, preferred_element_type=jnp.float32)
        up_act = jnp.dot(tok_rows, up_cols, preferred_element_type=jnp.float32)
        hidden = (jax.nn.silu(gate_act) * up_act).astype(jnp.bfloat16)
        partial_out = jnp.dot(hidden, down_rows, preferred_element_type=jnp.float32).astype(
            jnp.bfloat16
        )
        returned = lax.all_to_all(
            partial_out.reshape(received.shape), "expert", split_axis=0, concat_axis=0, tiled=True
        )
        fwd_back = returned[:, :CAP]
        rev_back = returned[:, CAP:]
        forward_now = shifted(finish_stream(forward_now, fwd_back, fwd_mix), "pipe", 1)
        reverse_now = shifted(finish_stream(reverse_now, rev_back, rev_mix), "pipe", -1)
    return (forward_now, reverse_now)


def relay_kernel(
    fwd_hbm,
    rev_hbm,
    gain_hbm,
    gate_hbm,
    up_hbm,
    down_hbm,
    routes_fwd_hbm,
    scores_fwd_hbm,
    routes_rev_hbm,
    scores_rev_hbm,
    fwd_out,
    rev_out,
    states,
    gain_ref,
    route_ref,
    score_ref,
    gate_up,
    down,
    table,
    table_in,
    early_out,
    early_in,
    slots,
    pieces,
    mate_pieces,
    chip_sums,
    returned,
    changed,
    changed_in,
    bulk_in,
    load_sem,
    table_send,
    table_recv,
    early_send,
    early_recv,
    slot_send,
    slot_recv,
    piece_send,
    piece_recv,
    back_send,
    back_recv,
    changed_send,
    changed_recv,
    bulk_send,
    bulk_recv,
):
    f32, bf16 = jnp.float32, jnp.bfloat16
    tokens, width = fwd_hbm.shape[1], fwd_hbm.shape[2]
    part = width // PARTS
    rows = PARTS * CAP
    sections = lax.axis_size("pipe")
    holders = lax.axis_size("expert")
    me_pipe = lax.axis_index("pipe")
    me_expert = lax.axis_index("expert")
    chips = holders // 2
    core = lax.rem(me_expert, 2)
    chip = me_expert // 2

    def at_section(offset):
        return {"pipe": lax.rem(me_pipe + sections + offset, sections)}

    def at_chip(offset):
        return {"expert": lax.rem(chip + chips + offset, chips) * 2 + core}

    mate = {"expert": chip * 2 + 1 - core}

    unsent = []

    def remote(source, target, send, recv, device):
        return pltpu.make_async_remote_copy(
            src_ref=source,
            dst_ref=target,
            send_sem=send,
            recv_sem=recv,
            device_id=device,
            device_id_type=MESH,
        )

    def launch(copy):
        copy.start()
        unsent.append(copy)

    barrier = pltpu.get_barrier_semaphore()
    peers = [at_section(d) for d in range(1, 4)] + [at_chip(k) for k in range(1, chips)] + [mate]
    for peer in peers:
        pl.semaphore_signal(barrier, inc=1, device_id=peer, device_id_type=MESH)

    loads = [
        (routes_fwd_hbm.at[:, 0], route_ref.at[0]),
        (routes_rev_hbm.at[:, 0], route_ref.at[1]),
        (scores_fwd_hbm.at[:, 0], score_ref.at[0]),
        (scores_rev_hbm.at[:, 0], score_ref.at[1]),
        (fwd_hbm.at[0], states.at[0]),
        (rev_hbm.at[0], states.at[1]),
        (gain_hbm, gain_ref),
        (gate_hbm.at[0], gate_up.at[:, 0:128]),
        (up_hbm.at[0], gate_up.at[:, 128:256]),
        (down_hbm.at[0], down),
    ]
    loads = [
        pltpu.make_async_copy(source, target, load_sem.at[i])
        for i, (source, target) in enumerate(loads)
    ]
    for copy in loads:
        copy.start()
    for copy in loads[:4]:
        copy.wait()

    before = (
        lax.broadcasted_iota(jnp.int32, (tokens, tokens), 0)
        <= lax.broadcasted_iota(jnp.int32, (tokens, tokens), 1)
    ).astype(f32)
    slot_of_row = lax.rem(lax.broadcasted_iota(jnp.int32, (8, tokens), 0), CAP).astype(f32)
    mix = {}
    for stream in range(2):
        for step in range(STEPS):
            match = (route_ref[stream, step] == 0).astype(f32)
            score = score_ref[stream, step]
            hit = jnp.sum(match, axis=0, keepdims=True)
            weighted = (
                ROUTE_SCALE
                * jnp.sum(match * score, axis=0, keepdims=True)
                / jnp.sum(score, axis=0, keepdims=True)
            )
            hits = jnp.broadcast_to(hit, (8, tokens))
            place = jnp.dot(hits, before, preferred_element_type=f32) - 1.0
            placed = hits * (place == slot_of_row).astype(f32)
            table[stream, step] = placed
            column = jnp.sum(placed * weighted, axis=1, keepdims=True)
            mix[stream, step] = jnp.concatenate([column, column], axis=0)

    part_of_row = lax.broadcasted_iota(jnp.int32, (rows, part), 0) // CAP

    def by_part(pick):
        total = pick(PARTS - 1)
        for q in range(PARTS - 1):
            total = jnp.where(part_of_row == q, pick(q), total)
        return total

    def cols(q):
        return slice(q * part, (q + 1) * part)

    def twice(placed):
        return jnp.concatenate([placed, placed], axis=0)

    def select(placed, state):
        marks = twice(placed).astype(bf16)
        return by_part(
            lambda q: jnp.dot(marks, state[:, cols(q)], preferred_element_type=f32)
        )

    for copy in loads[4:7]:
        copy.wait()
    gain = by_part(lambda q: jnp.broadcast_to(gain_ref[:, cols(q)], (rows, part)))

    def table_copy(d):
        return remote(
            table, table_in.at[d - 1], table_send.at[d - 1], table_recv.at[d - 1], at_section(d)
        )

    def sign(stream):
        return 1 if stream == 0 else -1

    def table_from(stream, behind):
        offset = behind if stream == 0 else (-behind) % 4
        return table_in.at[offset - 1, stream]

    def early_copy(stream, d):
        return remote(
            early_out.at[stream, d - 1],
            early_in.at[stream, d - 1],
            early_send.at[stream, d - 1],
            early_recv.at[stream, d - 1],
            at_section(sign(stream) * d),
        )

    def bulk_copy(stream, chunk):
        size = tokens * PARTS // CHUNKS
        piece = pl.ds(chunk // PARTS * size, size)
        piece = (stream, piece, pl.ds(chunk % PARTS * part, part))
        return remote(
            states.at[piece],
            bulk_in.at[piece],
            bulk_send.at[stream, chunk],
            bulk_recv.at[stream, chunk],
            at_section(sign(stream) * 3),
        )

    def changed_copy(stream, step, d):
        return remote(
            changed.at[stream, step],
            changed_in.at[stream, step, d - 1],
            changed_send.at[stream, step, d - 1],
            changed_recv.at[stream, step, d - 1],
            at_section(sign(stream) * d),
        )

    def slot_copy(stream, step, k):
        return remote(
            slots.at[stream, step, 0],
            slots.at[stream, step, k],
            slot_send.at[stream, step, k],
            slot_recv.at[stream, step, k],
            at_chip(k),
        )

    def mate_copy(stream, step, k):
        return remote(
            slots.at[stream, step, k],
            slots.at[stream, step, chips + k],
            slot_send.at[stream, step, chips + k],
            slot_recv.at[stream, step, chips + k],
            mate,
        )

    def piece_copy(stream, step):
        return remote(
            pieces.at[stream, step, 1],
            mate_pieces.at[stream, step],
            piece_send.at[stream, step],
            piece_recv.at[stream, step],
            mate,
        )

    def back_copy(stream, step, k):
        return remote(
            chip_sums.at[stream, step, k],
            returned.at[stream, step, k - 1],
            back_send.at[stream, step, k - 1],
            back_recv.at[stream, step, k - 1],
            at_chip(-k),
        )

    row_part = lax.broadcasted_iota(jnp.int32, (rows, rows), 0) // CAP
    col_part = lax.broadcasted_iota(jnp.int32, (rows, rows), 1) // CAP
    same_part = (row_part == col_part).astype(f32)

    def chain(stream):
        for step in range(STEPS):
            own = table[stream, step]
            if step == 0:
                current = select(own, states.at[stream])
            else:
                early_copy(stream, step).wait_recv()
                current = early_in[stream, step - 1].astype(f32)
                for past in range(step):
                    behind = step - past
                    match = same_part * lax.dot_general(
                        twice(own),
                        twice(table_from(stream, behind)[past]),
                        (((1,), (1,)), ((), ())),
                        preferred_element_type=f32,
                    )
                    seen = jnp.sum(match, axis=1, keepdims=True)
                    changed_copy(stream, past, behind).wait_recv()
                    newer = jnp.dot(
                        match.astype(bf16),
                        changed_in[stream, past, behind - 1],
                        preferred_element_type=f32,
                    )
                    current = jnp.where(seen > 0.5, newer, current)
            squares = jnp.sum(current * current, axis=1, keepdims=True)
            squares = jnp.broadcast_to(squares, (rows, 128))
            squares = squares[:8] + squares[8:]
            squares = squares + pltpu.roll(squares, 4, 0)
            factor = lax.rsqrt(squares[:, :1] * (1.0 / width) + EPSILON)
            slots[stream, step, 0] = (current * twice(factor) * gain).astype(bf16)
            if step == 0 and stream == 0:
                pl.semaphore_wait(barrier, len(peers))
                tables_out()
            for k in (2, 1, 3):
                launch(slot_copy(stream, step, k))
            launch(mate_copy(stream, step, 0))
            yield
            for k in (1, 3, 2):
                slot_copy(stream, step, k).wait_recv()
                launch(mate_copy(stream, step, k))
            yield
            for k in range(chips):
                mate_copy(stream, step, k).wait_recv()
            if step == 0 and stream == 0:
                for copy in loads[7:]:
                    copy.wait()
            gathered = slots[stream, step].reshape(holders * rows, part)
            total = None
            part_of_line = (
                lax.broadcasted_iota(jnp.int32, (holders * rows, 256), 0) % rows
            ) // CAP
            for q in range(PARTS):
                product = jnp.dot(gathered, gate_up[cols(q), :], preferred_element_type=f32)
                total = product if q == 0 else jnp.where(part_of_line == q, product, total)
            total = total.reshape(holders, 2, 8, 256)
            total = total[:, 0] + total[:, 1]
            total = (total + pltpu.roll(total, 4, 1)).reshape(holders * 8, 256)
            gate_act, up_act = total[:, :128], total[:, 128:]
            hidden = (gate_act / (1.0 + jnp.exp(-gate_act)) * up_act).astype(bf16)
            low = lax.broadcasted_iota(jnp.int32, (holders * 8, part), 0) % 8 < CAP
            halves = []
            for half in range(2):
                one = jnp.dot(hidden, down[:, cols(2 * half)], preferred_element_type=f32)
                two = jnp.dot(hidden, down[:, cols(2 * half + 1)], preferred_element_type=f32)
                halves.append(jnp.where(low, one, two).reshape(holders, 1, 8, part))
            joined = jnp.concatenate(halves, axis=1).reshape(2, chips, rows, part)
            pieces[stream, step] = joined.astype(bf16)
            launch(piece_copy(stream, step))
            yield
            piece_copy(stream, step).wait_recv()
            sums = pieces[stream, step, 0].astype(f32) + mate_pieces[stream, step].astype(f32)
            chip_sums[stream, step] = sums.astype(bf16)
            for k in (2, 1, 3):
                launch(back_copy(stream, step, k))
            yield
            expert_out = sums[0]
            for k in range(1, chips):
                back_copy(stream, step, k).wait_recv()
                expert_out = expert_out + returned[stream, step, k - 1].astype(f32)
            changed[stream, step] = (current + mix[stream, step] * expert_out).astype(bf16)
            launch(changed_copy(stream, step, 1))
            yield
            farther.extend((stream, step, d) for d in range(2, STEPS - step + 1))

    def tables_out():
        for d in range(1, 4):
            launch(table_copy(d))

    def early_rows():
        for d in range(1, 4):
            table_copy(d).wait_recv()
        for stream in range(2):
            for d in range(1, STEPS):
                ahead = table_from(stream, 4 - d)
                early_out[stream, d - 1] = select(ahead[d], states.at[stream]).astype(bf16)
                launch(early_copy(stream, d))

    farther = []
    later = [(stream, chunk) for chunk in range(CHUNKS) for stream in range(2)]
    chains = [chain(0), chain(1)]
    second = chains[1]
    next(chains[0])
    turn = 0
    while chains:
        for one in list(chains):
            try:
                next(one)
            except StopIteration:
                chains.remove(one)
            if one is second:
                for stream, step, d in farther:
                    launch(changed_copy(stream, step, d))
                farther.clear()
            if turn > 0:
                for stream, chunk in later[:2]:
                    launch(bulk_copy(stream, chunk))
                del later[:2]
        if turn == 0:
            early_rows()
        turn += 1

    lanes = 128
    slot_lane = lax.broadcasted_iota(jnp.int32, (tokens, lanes), 1)
    for stream, out in ((0, fwd_out), (1, rev_out)):
        marks = []
        for step in range(STEPS):
            placed = table_from(stream, STEPS - step)[step]
            for later in range(step + 1, STEPS):
                newer = table_from(stream, STEPS - later)[later]
                placed = placed * (1.0 - jnp.sum(newer[:CAP], axis=0, keepdims=True))
            marks.append(twice(placed))
        marks.append(jnp.zeros((lanes - STEPS * rows, tokens), f32))
        spread = jnp.concatenate(marks, axis=0).T
        seen = jnp.sum(spread, axis=1, keepdims=True) > 0.5
        for chunk in range(CHUNKS):
            bulk_copy(stream, chunk).wait_recv()
        for step in range(STEPS):
            changed_copy(stream, step, STEPS - step).wait_recv()
        newest = [changed_in[stream, step, STEPS - step - 1] for step in range(STEPS)]
        newest.append(jnp.zeros((lanes - STEPS * rows, part), bf16))
        newest = jnp.concatenate(newest, axis=0)
        for q in range(PARTS):
            chosen = jnp.where(lax.rem(slot_lane, rows) // CAP == q, spread, 0.0).astype(bf16)
            newer = jnp.dot(chosen, newest, preferred_element_type=f32)
            older = bulk_in[stream, :, cols(q)].astype(f32)
            out[0, :, cols(q)] = jnp.where(seen, newer, older).astype(bf16)

    for copy in unsent:
        copy.wait_send()


def relay_local(
    fwd_state,
    rev_state,
    norm_gain,
    w_gate,
    w_up,
    w_down,
    routes_fwd,
    scores_fwd,
    routes_rev,
    scores_rev,
):
    tokens, width = fwd_state.shape[1:]
    part = width // PARTS
    rows = PARTS * CAP
    holders = SPLIT
    chips = holders // 2
    bf16 = jnp.bfloat16

    in_hbm = pl.BlockSpec(memory_space=pltpu.HBM)
    vmem = pl.BlockSpec(memory_space=pltpu.VMEM)
    names = routes_fwd.shape[3]
    dma = pltpu.SemaphoreType.DMA
    return pl.pallas_call(
        relay_kernel,
        out_shape=[jax.ShapeDtypeStruct(fwd_state.shape, bf16)] * 2,
        in_specs=[in_hbm] * 10,
        out_specs=[vmem, vmem],
        scratch_shapes=[
            pltpu.VMEM((2, tokens, width), bf16),
            pltpu.VMEM((1, width), jnp.float32),
            pltpu.VMEM((2, STEPS, names, tokens), jnp.int32),
            pltpu.VMEM((2, STEPS, names, tokens), jnp.float32),
            pltpu.VMEM((width, 256), bf16),
            pltpu.VMEM((128, width), bf16),
            pltpu.VMEM((2, STEPS, 8, tokens), jnp.float32),
            pltpu.VMEM((3, 2, STEPS, 8, tokens), jnp.float32),
            pltpu.VMEM((2, STEPS - 1, rows, part), bf16),
            pltpu.VMEM((2, STEPS - 1, rows, part), bf16),
            pltpu.VMEM((2, STEPS, holders, rows, part), bf16),
            pltpu.VMEM((2, STEPS, 2, chips, rows, part), bf16),
            pltpu.VMEM((2, STEPS, chips, rows, part), bf16),
            pltpu.VMEM((2, STEPS, chips, rows, part), bf16),
            pltpu.VMEM((2, STEPS, chips - 1, rows, part), bf16),
            pltpu.VMEM((2, STEPS, rows, part), bf16),
            pltpu.VMEM((2, STEPS, STEPS, rows, part), bf16),
            pltpu.VMEM((2, tokens, width), bf16),
            dma((10,)),
            dma((3,)),
            dma((3,)),
            dma((2, STEPS - 1)),
            dma((2, STEPS - 1)),
            dma((2, STEPS, holders)),
            dma((2, STEPS, holders)),
            dma((2, STEPS)),
            dma((2, STEPS)),
            dma((2, STEPS, chips - 1)),
            dma((2, STEPS, chips - 1)),
            dma((2, STEPS, STEPS)),
            dma((2, STEPS, STEPS)),
            dma((2, CHUNKS)),
            dma((2, CHUNKS)),
        ],
        compiler_params=pltpu.CompilerParams(
            collective_id=0, has_side_effects=True, vmem_limit_bytes=64 * 1024 * 1024
        ),
        cost_estimate=pl.CostEstimate(
            flops=1_000_000_000, bytes_accessed=8_000_000, transcendentals=100_000
        ),
    )(
        fwd_state,
        rev_state,
        norm_gain,
        w_gate,
        w_up,
        w_down,
        *(x.transpose(0, 1, 3, 2) for x in (routes_fwd, scores_fwd, routes_rev, scores_rev)),
    )


def solution(mesh):
    in_specs = (
        P("pipe", "expert", None),
        P("pipe", "expert", None),
        P("pipe", None),
        P("pipe", None, "expert"),
        P("pipe", None, "expert"),
        P("pipe", "expert", None),
        P(None, "pipe", "expert", None),
        P(None, "pipe", "expert", None),
        P(None, "pipe", "expert", None),
        P(None, "pipe", "expert", None),
    )
    out_specs = (P("pipe", "expert", None), P("pipe", "expert", None))
    small = mesh.shape["pipe"] == 4 and mesh.shape["expert"] == SPLIT
    local = relay_local if small else general_local
    return jax.shard_map(local, mesh=mesh, in_specs=in_specs, out_specs=out_specs, check_vma=False)
```

```python
import jax
import jax.numpy as jnp
from jax import lax
from jax.experimental import pallas as pl
from jax.experimental.pallas import tpu as pltpu
from jax.sharding import PartitionSpec as P

SPLIT = 8
CAP = 4
STEPS = 3
PARTS = 4
CHUNKS = 16

EPSILON = 1e-06
ROUTE_SCALE = 2.5
MESH = pl.DeviceIdType.MESH


def shifted(value, axis, steps):
    count = lax.axis_size(axis)
    pairs = [(source, (source + steps) % count) for source in range(count)]
    return lax.ppermute(value, axis, pairs)


def normalize(tok_rows, gain_row):
    values = tok_rows.astype(jnp.float32)
    factor = lax.rsqrt(jnp.mean(values * values, axis=-1, keepdims=True) + EPSILON)
    return (values * factor * gain_row).astype(jnp.bfloat16)


def slot_tables(route_ids, route_scores, flying):
    expert_ids = jnp.arange(flying, dtype=jnp.int32)
    matches = (route_ids[:, :, None] == expert_ids[None, None, :]).astype(jnp.float32)
    hit_mask = jnp.sum(matches, axis=1)
    weighted = (
        ROUTE_SCALE
        * jnp.sum(matches * route_scores[:, :, None], axis=1)
        / jnp.sum(route_scores, axis=1, keepdims=True)
    )
    slot_index = jnp.cumsum(hit_mask, axis=0) - 1.0
    slot_ids = jnp.arange(CAP, dtype=jnp.float32)
    placed = hit_mask.T[:, None, :] * (slot_index.T[:, None, :] == slot_ids[None, :, None]).astype(
        jnp.float32
    )
    mix_table = placed * weighted.T[:, None, :]
    return (placed, mix_table)


def dispatch_slots(normed, placed):
    return jnp.einsum(
        "ecr,rd->ecd", placed, normed.astype(jnp.float32), precision=lax.Precision.HIGHEST
    ).astype(jnp.bfloat16)


def finish(tok_rows, summed, mix_table):
    added = jnp.einsum("ecr,ecd->rd", mix_table, summed, precision=lax.Precision.HIGHEST)
    return (tok_rows.astype(jnp.float32) + added).astype(jnp.bfloat16)


def general_local(
    fwd_state,
    rev_state,
    norm_gain,
    w_gate,
    w_up,
    w_down,
    routes_fwd,
    scores_fwd,
    routes_rev,
    scores_rev,
):
    flying = lax.axis_size("expert") // SPLIT
    width = fwd_state.shape[2]
    gain_row = norm_gain[0]
    gate_cols = w_gate[0]
    up_cols = w_up[0]
    down_rows = w_down[0]

    def prepare(current, route_ids, route_scores):
        normed = normalize(current[0], gain_row)
        placed, mix_table = slot_tables(route_ids, route_scores, flying)
        slot_rows = dispatch_slots(normed, placed)
        copies = jnp.broadcast_to(slot_rows[:, None], (flying, SPLIT, CAP, width)).reshape(
            flying * SPLIT, CAP, width
        )
        return (copies, mix_table)

    def finish_stream(current, returned, mix_table):
        summed = jnp.sum(returned.astype(jnp.float32).reshape(flying, SPLIT, CAP, width), axis=1)
        return finish(current[0], summed, mix_table)[None]

    forward_now = fwd_state
    reverse_now = rev_state
    for step_index in range(STEPS):
        fwd_copies, fwd_mix = prepare(
            forward_now, routes_fwd[step_index, 0], scores_fwd[step_index, 0]
        )
        rev_copies, rev_mix = prepare(
            reverse_now, routes_rev[step_index, 0], scores_rev[step_index, 0]
        )
        joined = jnp.concatenate([fwd_copies, rev_copies], axis=1)
        received = lax.all_to_all(joined, "expert", split_axis=0, concat_axis=0, tiled=True)
        tok_rows = received.reshape(-1, width)
        gate_act = jnp.dot(tok_rows, gate_cols, preferred_element_type=jnp.float32)
        up_act = jnp.dot(tok_rows, up_cols, preferred_element_type=jnp.float32)
        hidden = (jax.nn.silu(gate_act) * up_act).astype(jnp.bfloat16)
        partial_out = jnp.dot(hidden, down_rows, preferred_element_type=jnp.float32).astype(
            jnp.bfloat16
        )
        returned = lax.all_to_all(
            partial_out.reshape(received.shape), "expert", split_axis=0, concat_axis=0, tiled=True
        )
        fwd_back = returned[:, :CAP]
        rev_back = returned[:, CAP:]
        forward_now = shifted(finish_stream(forward_now, fwd_back, fwd_mix), "pipe", 1)
        reverse_now = shifted(finish_stream(reverse_now, rev_back, rev_mix), "pipe", -1)
    return (forward_now, reverse_now)


def relay_kernel(
    fwd_hbm,
    rev_hbm,
    gain_hbm,
    gate_hbm,
    up_hbm,
    down_hbm,
    routes_fwd_hbm,
    scores_fwd_hbm,
    routes_rev_hbm,
    scores_rev_hbm,
    fwd_moved,
    rev_moved,
    spread_out,
    newest_out,
    states,
    gain_ref,
    route_ref,
    score_ref,
    gate_up,
    down,
    table,
    table_in,
    early_out,
    early_in,
    slots,
    pieces,
    mate_pieces,
    chip_sums,
    returned,
    changed,
    changed_in,
    load_sem,
    table_send,
    table_recv,
    early_send,
    early_recv,
    slot_send,
    slot_recv,
    piece_send,
    piece_recv,
    back_send,
    back_recv,
    changed_send,
    changed_recv,
    bulk_send,
    bulk_recv,
):
    f32, bf16 = jnp.float32, jnp.bfloat16
    tokens, width = fwd_hbm.shape[1], fwd_hbm.shape[2]
    part = width // PARTS
    rows = PARTS * CAP
    sections = lax.axis_size("pipe")
    holders = lax.axis_size("expert")
    me_pipe = lax.axis_index("pipe")
    me_expert = lax.axis_index("expert")
    chips = holders // 2
    core = lax.rem(me_expert, 2)
    chip = me_expert // 2

    def at_section(offset):
        return {"pipe": lax.rem(me_pipe + sections + offset, sections)}

    def at_chip(offset):
        return {"expert": lax.rem(chip + chips + offset, chips) * 2 + core}

    mate = {"expert": chip * 2 + 1 - core}

    unsent = []

    def remote(source, target, send, recv, device):
        return pltpu.make_async_remote_copy(
            src_ref=source,
            dst_ref=target,
            send_sem=send,
            recv_sem=recv,
            device_id=device,
            device_id_type=MESH,
        )

    def launch(copy):
        copy.start()
        unsent.append(copy)

    barrier = pltpu.get_barrier_semaphore()
    peers = [at_section(d) for d in range(1, 4)] + [at_chip(k) for k in range(1, chips)] + [mate]
    for peer in peers:
        pl.semaphore_signal(barrier, inc=1, device_id=peer, device_id_type=MESH)

    loads = [
        (routes_fwd_hbm.at[:, 0], route_ref.at[0]),
        (routes_rev_hbm.at[:, 0], route_ref.at[1]),
        (scores_fwd_hbm.at[:, 0], score_ref.at[0]),
        (scores_rev_hbm.at[:, 0], score_ref.at[1]),
        (fwd_hbm.at[0], states.at[0]),
        (rev_hbm.at[0], states.at[1]),
        (gain_hbm, gain_ref),
        (gate_hbm.at[0], gate_up.at[:, 0:128]),
        (up_hbm.at[0], gate_up.at[:, 128:256]),
        (down_hbm.at[0], down),
    ]
    loads = [
        pltpu.make_async_copy(source, target, load_sem.at[i])
        for i, (source, target) in enumerate(loads)
    ]
    for copy in loads:
        copy.start()
    for copy in loads[:4]:
        copy.wait()

    before = (
        lax.broadcasted_iota(jnp.int32, (tokens, tokens), 0)
        <= lax.broadcasted_iota(jnp.int32, (tokens, tokens), 1)
    ).astype(f32)
    slot_of_row = lax.rem(lax.broadcasted_iota(jnp.int32, (8, tokens), 0), CAP).astype(f32)
    mix = {}
    for stream in range(2):
        for step in range(STEPS):
            match = (route_ref[stream, step] == 0).astype(f32)
            score = score_ref[stream, step]
            hit = jnp.sum(match, axis=0, keepdims=True)
            weighted = (
                ROUTE_SCALE
                * jnp.sum(match * score, axis=0, keepdims=True)
                / jnp.sum(score, axis=0, keepdims=True)
            )
            hits = jnp.broadcast_to(hit, (8, tokens))
            place = jnp.dot(hits, before, preferred_element_type=f32) - 1.0
            placed = hits * (place == slot_of_row).astype(f32)
            table[stream, step] = placed
            column = jnp.sum(placed * weighted, axis=1, keepdims=True)
            mix[stream, step] = jnp.concatenate([column, column], axis=0)

    part_of_row = lax.broadcasted_iota(jnp.int32, (rows, part), 0) // CAP

    def by_part(pick):
        total = pick(PARTS - 1)
        for q in range(PARTS - 1):
            total = jnp.where(part_of_row == q, pick(q), total)
        return total

    def cols(q):
        return slice(q * part, (q + 1) * part)

    def twice(placed):
        return jnp.concatenate([placed, placed], axis=0)

    def select(placed, state):
        marks = twice(placed).astype(bf16)
        return by_part(
            lambda q: jnp.dot(marks, state[:, cols(q)], preferred_element_type=f32)
        )

    for copy in loads[4:7]:
        copy.wait()
    gain = by_part(lambda q: jnp.broadcast_to(gain_ref[:, cols(q)], (rows, part)))

    def table_copy(d):
        return remote(
            table, table_in.at[d - 1], table_send.at[d - 1], table_recv.at[d - 1], at_section(d)
        )

    def sign(stream):
        return 1 if stream == 0 else -1

    def table_from(stream, behind):
        offset = behind if stream == 0 else (-behind) % 4
        return table_in.at[offset - 1, stream]

    def early_copy(stream, d):
        return remote(
            early_out.at[stream, d - 1],
            early_in.at[stream, d - 1],
            early_send.at[stream, d - 1],
            early_recv.at[stream, d - 1],
            at_section(sign(stream) * d),
        )

    def bulk_copy(stream, chunk):
        size = tokens * PARTS // CHUNKS
        piece = pl.ds(chunk // PARTS * size, size)
        columns = pl.ds(chunk % PARTS * part, part)
        return remote(
            states.at[stream, piece, columns],
            (fwd_moved, rev_moved)[stream].at[0, piece, columns],
            bulk_send.at[stream, chunk],
            bulk_recv.at[stream, chunk],
            at_section(sign(stream) * 3),
        )

    def changed_copy(stream, step, d):
        return remote(
            changed.at[stream, step],
            changed_in.at[stream, step, d - 1],
            changed_send.at[stream, step, d - 1],
            changed_recv.at[stream, step, d - 1],
            at_section(sign(stream) * d),
        )

    def slot_copy(stream, step, k):
        return remote(
            slots.at[stream, step, 0],
            slots.at[stream, step, k],
            slot_send.at[stream, step, k],
            slot_recv.at[stream, step, k],
            at_chip(k),
        )

    def mate_copy(stream, step, k):
        return remote(
            slots.at[stream, step, k],
            slots.at[stream, step, chips + k],
            slot_send.at[stream, step, chips + k],
            slot_recv.at[stream, step, chips + k],
            mate,
        )

    def piece_copy(stream, step):
        return remote(
            pieces.at[stream, step, 1],
            mate_pieces.at[stream, step],
            piece_send.at[stream, step],
            piece_recv.at[stream, step],
            mate,
        )

    def back_copy(stream, step, k):
        return remote(
            chip_sums.at[stream, step, k],
            returned.at[stream, step, k - 1],
            back_send.at[stream, step, k - 1],
            back_recv.at[stream, step, k - 1],
            at_chip(-k),
        )

    row_part = lax.broadcasted_iota(jnp.int32, (rows, rows), 0) // CAP
    col_part = lax.broadcasted_iota(jnp.int32, (rows, rows), 1) // CAP
    same_part = (row_part == col_part).astype(f32)

    def chain(stream):
        for step in range(STEPS):
            own = table[stream, step]
            if step == 0:
                current = select(own, states.at[stream])
            else:
                early_copy(stream, step).wait_recv()
                current = early_in[stream, step - 1].astype(f32)
                for past in range(step):
                    behind = step - past
                    match = same_part * lax.dot_general(
                        twice(own),
                        twice(table_from(stream, behind)[past]),
                        (((1,), (1,)), ((), ())),
                        preferred_element_type=f32,
                    )
                    seen = jnp.sum(match, axis=1, keepdims=True)
                    changed_copy(stream, past, behind).wait_recv()
                    newer = jnp.dot(
                        match.astype(bf16),
                        changed_in[stream, past, behind - 1],
                        preferred_element_type=f32,
                    )
                    current = jnp.where(seen > 0.5, newer, current)
            squares = jnp.sum(current * current, axis=1, keepdims=True)
            squares = jnp.broadcast_to(squares, (rows, 128))
            squares = squares[:8] + squares[8:]
            squares = squares + pltpu.roll(squares, 4, 0)
            factor = lax.rsqrt(squares[:, :1] * (1.0 / width) + EPSILON)
            slots[stream, step, 0] = (current * twice(factor) * gain).astype(bf16)
            if step == 0 and stream == 0:
                pl.semaphore_wait(barrier, len(peers))
                tables_out()
            for k in (2, 1, 3):
                launch(slot_copy(stream, step, k))
            launch(mate_copy(stream, step, 0))
            yield
            for k in (1, 3, 2):
                slot_copy(stream, step, k).wait_recv()
                launch(mate_copy(stream, step, k))
            yield
            for k in range(chips):
                mate_copy(stream, step, k).wait_recv()
            if step == 0 and stream == 0:
                for copy in loads[7:]:
                    copy.wait()
            gathered = slots[stream, step].reshape(holders * rows, part)
            total = None
            part_of_line = (
                lax.broadcasted_iota(jnp.int32, (holders * rows, 256), 0) % rows
            ) // CAP
            for q in range(PARTS):
                product = jnp.dot(gathered, gate_up[cols(q), :], preferred_element_type=f32)
                total = product if q == 0 else jnp.where(part_of_line == q, product, total)
            total = total.reshape(holders, 2, 8, 256)
            total = total[:, 0] + total[:, 1]
            total = (total + pltpu.roll(total, 4, 1)).reshape(holders * 8, 256)
            gate_act, up_act = total[:, :128], total[:, 128:]
            hidden = (gate_act / (1.0 + jnp.exp(-gate_act)) * up_act).astype(bf16)
            low = lax.broadcasted_iota(jnp.int32, (holders * 8, part), 0) % 8 < CAP
            halves = []
            for half in range(2):
                one = jnp.dot(hidden, down[:, cols(2 * half)], preferred_element_type=f32)
                two = jnp.dot(hidden, down[:, cols(2 * half + 1)], preferred_element_type=f32)
                halves.append(jnp.where(low, one, two).reshape(holders, 1, 8, part))
            joined = jnp.concatenate(halves, axis=1).reshape(2, chips, rows, part)
            pieces[stream, step] = joined.astype(bf16)
            launch(piece_copy(stream, step))
            yield
            piece_copy(stream, step).wait_recv()
            sums = pieces[stream, step, 0].astype(f32) + mate_pieces[stream, step].astype(f32)
            chip_sums[stream, step] = sums.astype(bf16)
            for k in (2, 1, 3):
                launch(back_copy(stream, step, k))
            yield
            expert_out = sums[0]
            for k in range(1, chips):
                back_copy(stream, step, k).wait_recv()
                expert_out = expert_out + returned[stream, step, k - 1].astype(f32)
            changed[stream, step] = (current + mix[stream, step] * expert_out).astype(bf16)
            launch(changed_copy(stream, step, 1))
            yield
            farther.extend((stream, step, d) for d in range(2, STEPS - step + 1))

    def tables_out():
        for d in range(1, 4):
            launch(table_copy(d))

    def early_rows():
        for d in range(1, 4):
            table_copy(d).wait_recv()
        for stream in range(2):
            for d in range(1, STEPS):
                ahead = table_from(stream, 4 - d)
                early_out[stream, d - 1] = select(ahead[d], states.at[stream]).astype(bf16)
                launch(early_copy(stream, d))

    def spread_tables():
        for stream in range(2):
            marks = []
            for step in range(STEPS):
                placed = table_from(stream, STEPS - step)[step]
                for after in range(step + 1, STEPS):
                    newer = table_from(stream, STEPS - after)[after]
                    placed = placed * (1.0 - jnp.sum(newer[:CAP], axis=0, keepdims=True))
                marks.append(twice(placed))
            rest = spread_out.shape[2] - STEPS * rows
            marks.append(jnp.zeros((rest, tokens), f32))
            spread_out[stream] = jnp.concatenate(marks, axis=0).T
            newest_out[stream, STEPS * rows :] = jnp.zeros((rest, part), bf16)

    farther = []
    later = [(stream, chunk) for chunk in range(CHUNKS) for stream in range(2)]
    chains = [chain(0), chain(1)]
    second = chains[1]
    next(chains[0])
    turn = 0
    while chains:
        for one in list(chains):
            try:
                next(one)
            except StopIteration:
                chains.remove(one)
            if one is second:
                for stream, step, d in farther:
                    launch(changed_copy(stream, step, d))
                farther.clear()
            pieces_now = 2 if turn % 2 == 1 and one is not second else 1
            for stream, chunk in later[:pieces_now]:
                launch(bulk_copy(stream, chunk))
            del later[:pieces_now]
        if turn == 0:
            early_rows()
        if turn == 3:
            spread_tables()
        turn += 1
    assert not later

    for stream in range(2):
        for chunk in range(CHUNKS):
            bulk_copy(stream, chunk).wait_recv()
        for step in range(STEPS):
            changed_copy(stream, step, STEPS - step).wait_recv()
            newest_out[stream, rows * step : rows * (step + 1)] = changed_in[
                stream, step, STEPS - step - 1
            ]

    for copy in unsent:
        copy.wait_send()


def merge_kernel(fwd_moved, rev_moved, spread_ref, newest_ref, fwd_out, rev_out):
    q = pl.program_id(0)
    rows = PARTS * CAP
    for stream, moved, out in ((0, fwd_moved, fwd_out), (1, rev_moved, rev_out)):
        spread = spread_ref[stream]
        seen = jnp.sum(spread, axis=1, keepdims=True) > 0.5
        slot_lane = lax.broadcasted_iota(jnp.int32, spread.shape, 1)
        chosen = jnp.where(lax.rem(slot_lane, rows) // CAP == q, spread, 0.0)
        newer = jnp.dot(
            chosen.astype(jnp.bfloat16), newest_ref[stream], preferred_element_type=jnp.float32
        )
        out[0] = jnp.where(seen, newer, moved[0].astype(jnp.float32)).astype(jnp.bfloat16)


def relay_local(
    fwd_state,
    rev_state,
    norm_gain,
    w_gate,
    w_up,
    w_down,
    routes_fwd,
    scores_fwd,
    routes_rev,
    scores_rev,
):
    tokens, width = fwd_state.shape[1:]
    part = width // PARTS
    rows = PARTS * CAP
    holders = SPLIT
    chips = holders // 2
    bf16 = jnp.bfloat16

    in_hbm = pl.BlockSpec(memory_space=pltpu.HBM)
    vmem = pl.BlockSpec(memory_space=pltpu.VMEM)
    names = routes_fwd.shape[3]
    dma = pltpu.SemaphoreType.DMA
    moved = [jax.ShapeDtypeStruct(fwd_state.shape, bf16)] * 2
    fwd_moved, rev_moved, spread, newest = pl.pallas_call(
        relay_kernel,
        out_shape=moved
        + [
            jax.ShapeDtypeStruct((2, tokens, 128), jnp.float32),
            jax.ShapeDtypeStruct((2, 128, part), bf16),
        ],
        in_specs=[in_hbm] * 10,
        out_specs=[in_hbm, in_hbm, vmem, vmem],
        scratch_shapes=[
            pltpu.VMEM((2, tokens, width), bf16),
            pltpu.VMEM((1, width), jnp.float32),
            pltpu.VMEM((2, STEPS, names, tokens), jnp.int32),
            pltpu.VMEM((2, STEPS, names, tokens), jnp.float32),
            pltpu.VMEM((width, 256), bf16),
            pltpu.VMEM((128, width), bf16),
            pltpu.VMEM((2, STEPS, 8, tokens), jnp.float32),
            pltpu.VMEM((3, 2, STEPS, 8, tokens), jnp.float32),
            pltpu.VMEM((2, STEPS - 1, rows, part), bf16),
            pltpu.VMEM((2, STEPS - 1, rows, part), bf16),
            pltpu.VMEM((2, STEPS, holders, rows, part), bf16),
            pltpu.VMEM((2, STEPS, 2, chips, rows, part), bf16),
            pltpu.VMEM((2, STEPS, chips, rows, part), bf16),
            pltpu.VMEM((2, STEPS, chips, rows, part), bf16),
            pltpu.VMEM((2, STEPS, chips - 1, rows, part), bf16),
            pltpu.VMEM((2, STEPS, rows, part), bf16),
            pltpu.VMEM((2, STEPS, STEPS, rows, part), bf16),
            dma((10,)),
            dma((3,)),
            dma((3,)),
            dma((2, STEPS - 1)),
            dma((2, STEPS - 1)),
            dma((2, STEPS, holders)),
            dma((2, STEPS, holders)),
            dma((2, STEPS)),
            dma((2, STEPS)),
            dma((2, STEPS, chips - 1)),
            dma((2, STEPS, chips - 1)),
            dma((2, STEPS, STEPS)),
            dma((2, STEPS, STEPS)),
            dma((2, CHUNKS)),
            dma((2, CHUNKS)),
        ],
        compiler_params=pltpu.CompilerParams(
            collective_id=0, has_side_effects=True, vmem_limit_bytes=64 * 1024 * 1024
        ),
        cost_estimate=pl.CostEstimate(
            flops=1_000_000_000, bytes_accessed=8_000_000, transcendentals=100_000
        ),
    )(
        fwd_state,
        rev_state,
        norm_gain,
        w_gate,
        w_up,
        w_down,
        *(x.transpose(0, 1, 3, 2) for x in (routes_fwd, scores_fwd, routes_rev, scores_rev)),
    )
    block = pl.BlockSpec((1, tokens, part), lambda q: (0, 0, q))
    return pl.pallas_call(
        merge_kernel,
        grid=(PARTS,),
        out_shape=moved,
        in_specs=[
            block,
            block,
            pl.BlockSpec(spread.shape, lambda q: (0, 0, 0)),
            pl.BlockSpec(newest.shape, lambda q: (0, 0, 0)),
        ],
        out_specs=[block, block],
        compiler_params=pltpu.CompilerParams(vmem_limit_bytes=64 * 1024 * 1024),
    )(fwd_moved, rev_moved, spread, newest)


def solution(mesh):
    in_specs = (
        P("pipe", "expert", None),
        P("pipe", "expert", None),
        P("pipe", None),
        P("pipe", None, "expert"),
        P("pipe", None, "expert"),
        P("pipe", "expert", None),
        P(None, "pipe", "expert", None),
        P(None, "pipe", "expert", None),
        P(None, "pipe", "expert", None),
        P(None, "pipe", "expert", None),
    )
    out_specs = (P("pipe", "expert", None), P("pipe", "expert", None))
    small = mesh.shape["pipe"] == 4 and mesh.shape["expert"] == SPLIT
    local = relay_local if small else general_local
    return jax.shard_map(local, mesh=mesh, in_specs=in_specs, out_specs=out_specs, check_vma=False)
```
